32 devices in a mesh: space: 16 (over z, y, x), rep: 2 (over core).
Axes of the slice: x: 2, y: 2, z: 4, core: 2. Of those that a mesh axis runs over, the one named last changes fastest.
Arguments:
- acts: bfloat16 [384, 512, 128], P(('space', 'rep')), may hold values from -6 to 6
- preact: bfloat16 [384, 512, 128], P(('space', 'rep')), may hold values from -8 to 8
- cotangent: bfloat16 [384, 512, 128], P(('space', 'rep')), may hold values from -6 to 6
- filt: bfloat16 [3456, 128], P('space', 'rep'), may hold values from -0.109375 to 0.109375
- counts: int32 [32], replicated, may hold values from 1 to 12, as said below
- neighbors: int32 [384, 27], P(('space', 'rep')), may hold values from 0 to 384, as said below
Outputs:
- input_grad: bfloat16 [384, 512, 128], P(('space', 'rep'))
- filt_grad: float32 [3456, 128], P('space', 'rep')
The draws below stay inside these ranges and needn't reach their ends.
Inputs may be any that keep to these rules, and one draw needn't show every extreme that they name: counts[d] is the number of live bricks of device d, which fill its first slots; counts[d] + counts[d xor 1] <= 16, where d xor 1 is the other core of the same chip; in every draw some device holds 12 bricks and its partner 2 * 8 - 12. Brick n = d * 12 + s sits in slab d of the brick grid at one of 5 x 5 places, slot 0 of every device at the middle place; neighbors[n, k] is the index of the live brick at offset off_k (first component along the slabs, so it lies on device d - 1, d or d + 1) from that place, or 384 where there is none, also for bricks that are not live.
All inputs are finite; a program needn't handle non-finite values.
Results may differ from the reference program's by a relative error of at most 0.0049.
Values may be sent and summed in bfloat16 or wider, within the bound.
No kernel may reach another device: no remote copies, remote signals or barrier semaphores. Data moves between devices by JAX's collectives and lax.ppermute only.
A program may use at most 128 MiB of HBM per device.

```python
import math
import jax
import jax.numpy as jnp
from jax import lax

C = 128
BRICK = 8
SIDE = 5
SLOTS = 12
KEEP = 8
VOX = 512
BRICKS = 384


def brick_layout(key):
    devices = BRICKS // SLOTS
    halves = devices // 2
    base_key = jax.random.fold_in(key, 7)
    key_total, key_split, key_pinned, key_flip, key_perm = jax.random.split(base_key, 5)
    pair_index = jnp.arange(halves)
    pinned = jax.random.randint(key_pinned, (), 0, halves)
    pair_total = jax.random.randint(key_total, (halves,), 2, 2 * KEEP + 1)
    pair_total = jnp.where(pair_index == pinned, 2 * KEEP, pair_total)
    lowest = jnp.maximum(1, pair_total - SLOTS)
    highest = jnp.minimum(SLOTS, pair_total - 1)
    first_share = jax.random.randint(key_split, (halves,), lowest, highest + 1)
    first_share = jnp.where(pair_index == pinned, SLOTS, first_share)
    second = pair_total - first_share
    flipped = jax.random.randint(key_flip, (halves,), 0, 2) == 1
    low_part = jnp.where(flipped, second, first_share)
    high_part = jnp.where(flipped, first_share, second)
    counts = jnp.stack([low_part, high_part], axis=1).reshape(devices).astype(jnp.int32)
    middle = SIDE * SIDE // 2
    device_keys = jax.random.split(key_perm, devices)
    others = jax.vmap(lambda key_one: jax.random.permutation(key_one, SIDE * SIDE - 1))(device_keys).astype(jnp.int32)
    others = others + (others >= middle).astype(jnp.int32)
    places = jnp.concatenate([jnp.full((devices, 1), middle, jnp.int32), others], axis=1).astype(jnp.int32)
    occupant = jnp.zeros((devices, SIDE * SIDE), jnp.int32).at[jnp.arange(devices)[:, None], places].set(jnp.arange(SIDE * SIDE, dtype=jnp.int32)[None, :])
    placed = places[:, :SLOTS]
    taps = jnp.arange(27)
    step_x = taps // 9 - 1
    step_y = taps // 3 % 3 - 1
    step_z = taps % 3 - 1
    target_dev = jnp.arange(devices)[:, None, None] + step_x[None, None, :]
    target_row = placed[:, :, None] // SIDE + step_y[None, None, :]
    target_col = placed[:, :, None] % SIDE + step_z[None, None, :]
    inside = (target_dev >= 0) & (target_dev < devices) & (target_row >= 0) & (target_row < SIDE) & (target_col >= 0) & (target_col < SIDE)
    clipped_dev = jnp.clip(target_dev, 0, devices - 1)
    clipped_row = jnp.clip(target_row, 0, SIDE - 1)
    clipped_col = jnp.clip(target_col, 0, SIDE - 1)
    target_slot = occupant[clipped_dev, clipped_row * SIDE + clipped_col]
    alive = inside & (target_slot < counts[clipped_dev])
    neighbor_table = jnp.where(alive, clipped_dev * SLOTS + target_slot, BRICKS).astype(jnp.int32)
    return (counts, neighbor_table.reshape(BRICKS, 27))


def draw_counts(key, part):
    return brick_layout(key)[0]


def draw_neighbors(key, part):
    return brick_layout(key)[1]


def levels(key, extent, cuts, least, largest):
    def one(dim, blocks):
        steps = jax.random.uniform(jax.random.fold_in(jax.random.fold_in(key, 6), dim), (blocks,), jnp.float32, least / len(cuts), largest / len(cuts))
        return jnp.repeat(jnp.exp(steps), extent[dim] // blocks).reshape((-1,) + (1,) * (len(extent) - dim - 1))

    gain = one(*cuts[0])
    for cut in cuts[1:]:
        gain = gain * one(*cut)
    return gain


def scatter_about(stream_key, extent, scale, most, pieces=(), kind=jnp.bfloat16):
    factor_of = levels(stream_key, extent, pieces, -0.22, 0.18) if pieces else 1.0
    drawn = jax.random.normal(stream_key, extent, jnp.float32) * scale * factor_of
    return jnp.minimum(jnp.maximum(drawn, -most), most).astype(kind)


def setup_inputs(seed: int = 0) -> dict:
    key_of = jax.random.split(jax.random.key(seed), 7)
    acts = scatter_about(key_of[0], (BRICKS, VOX, C), 1.0, 6.0, ((0, 32),))
    preact = scatter_about(key_of[1], (BRICKS, VOX, C), 1.5, 8.0, ((0, 32),))
    cotangent = scatter_about(key_of[2], (BRICKS, VOX, C), 1.0, 6.0, ((0, 32),))
    filt = scatter_about(key_of[3], (27 * C, C), (27 * C) ** -0.5, 0.109375, ((0, 16), (1, 2)))
    counts = draw_counts(jax.random.fold_in(key_of[6], 71), 0)
    neighbors = draw_neighbors(jax.random.fold_in(key_of[6], 71), 0)
    return {"acts": acts, "preact": preact, "cotangent": cotangent, "filt": filt, "counts": counts, "neighbors": neighbors}


tap_offsets = [(step_x, step_y, step_z) for step_x in (-1, 0, 1) for step_y in (-1, 0, 1) for step_z in (-1, 0, 1)]

def silu_slope(values):
    sigma = jax.nn.sigmoid(values)
    return sigma * (1.0 + values * (1.0 - sigma))

def edge(offset, brick_side):
    if offset < 0:
        return slice(brick_side - 1, brick_side)
    if offset == 0:
        return slice(0, brick_side)
    return slice(0, 1)

def assemble(planes, indices, usable):
    layers = []
    for step_x in range(3):
        strips = []
        for step_y in range(3):
            columns = []
            for step_z in range(3):
                tap = step_x * 9 + step_y * 3 + step_z
                source = planes[step_x]
                brick_side = source.shape[2]
                fetched = jnp.take(source, indices[:, tap], axis=0)
                fetched = fetched[:, :, edge(step_y - 1, brick_side), edge(step_z - 1, brick_side)]
                keeper = usable[:, tap][:, None, None, None, None]
                columns.append(jnp.where(keeper, fetched, jnp.zeros_like(fetched)))
            strips.append(jnp.concatenate(columns, axis=3))
        layers.append(jnp.concatenate(strips, axis=2))
    return jnp.concatenate(layers, axis=1)

def unfold(padded, direction):
    brick_side = padded.shape[0] - 2
    sections = []
    for step_x, step_y, step_z in tap_offsets:
        start_x = 1 + direction * step_x
        start_y = 1 + direction * step_y
        start_z = 1 + direction * step_z
        sections.append(padded[start_x:start_x + brick_side, start_y:start_y + brick_side, start_z:start_z + brick_side])
    return jnp.concatenate(sections, axis=-1).reshape(brick_side ** 3, -1)

def run_bricks(act_pad, grad_pad, filt_flip, running):

    def per_brick(accum, operands):
        act_block, grad_block = operands
        unrolled_act = unfold(act_block, 1)
        unrolled_grad = unfold(grad_block, -1)
        center = grad_block[1:-1, 1:-1, 1:-1].reshape(-1, grad_block.shape[-1])
        accum = accum + lax.dot_general(unrolled_act, center, (((0,), (0,)), ((), ())), preferred_element_type=jnp.float32)
        return (accum, jnp.dot(unrolled_grad, filt_flip, preferred_element_type=jnp.float32))
    return lax.scan(per_brick, running, (act_pad, grad_pad))

def reference(acts, preact, cotangent, filt, counts, neighbors):
    channels = acts.shape[2]
    devices = BRICKS // SLOTS
    is_live = jnp.arange(BRICKS) % SLOTS < jnp.repeat(counts, SLOTS)
    grad_pre = jnp.where(is_live[:, None, None], cotangent.astype(jnp.float32) * silu_slope(preact.astype(jnp.float32)), 0.0).astype(jnp.bfloat16)
    act_five = acts.reshape(BRICKS, BRICK, BRICK, BRICK, channels)
    grad_five = grad_pre.reshape(BRICKS, BRICK, BRICK, BRICK, channels)
    act_planes = (act_five[:, BRICK - 1:], act_five, act_five[:, :1])
    grad_planes = (grad_five[:, BRICK - 1:], grad_five, grad_five[:, :1])
    filt_flip = filt.reshape(27, channels, channels).transpose(0, 2, 1).reshape(27 * channels, channels)
    usable = neighbors < BRICKS
    indices = jnp.minimum(neighbors, BRICKS - 1).astype(jnp.int32)

    def per_device(running, operands):
        device_indices, device_usable = operands
        act_pad = assemble(act_planes, device_indices, device_usable)
        grad_pad = assemble(grad_planes, device_indices, device_usable)
        running, grads = run_bricks(act_pad, grad_pad, filt_flip, running)
        return (running, grads)
    start = jnp.zeros((27 * channels, channels), jnp.float32)
    filt_sum, grads = lax.scan(per_device, start, (indices.reshape(devices, SLOTS, 27), usable.reshape(devices, SLOTS, 27)))
    grads = grads.reshape(BRICKS, VOX, channels)
    input_grad = jnp.where(is_live[:, None, None], grads, 0.0).astype(jnp.bfloat16)
    return (input_grad, filt_sum * (1.0 / math.sqrt(BRICKS * VOX)))
```

```python
import functools
import math

import jax
import jax.numpy as jnp
from jax import lax
from jax.experimental import pallas as pl
from jax.experimental.pallas import tpu as pltpu
from jax.sharding import PartitionSpec as P

f32 = jnp.float32
bf16 = jnp.bfloat16
AXES = ("space", "rep")
LANES = 128


def silu_slope(values):
    sigma = jax.nn.sigmoid(values)
    return sigma * (1.0 + values * (1.0 - sigma))


def gated(preact, cotangent):
    return (cotangent.astype(f32) * silu_slope(preact.astype(f32))).astype(bf16)


def shifted(x, by):
    count = lax.axis_size(AXES)
    pairs = [(i, i + by) for i in range(count) if 0 <= i + by < count]
    return lax.ppermute(x, AXES, pairs)


def swapped(x, axis, mask):
    count = lax.axis_size(axis)
    return lax.ppermute(x, axis, [(i, i ^ mask) for i in range(count)])


def steps_of(count):
    out, unit = [], 1
    while unit < count:
        members = min(4, count // unit)
        out.append((unit, members))
        unit *= members
    return out


def neighbour_slots(nb_ref, brick, layer, position, slots, total, live):
    base = (position + (layer - 1)) * slots
    table = []
    for dy in range(3):
        row = []
        for dz in range(3):
            value = nb_ref[brick, layer * 9 + dy * 3 + dz]
            row.append(jnp.where((value >= total) | (brick >= live), slots, value - base))
        table.append(row)
    return table


def fill(unrolled, row, source, plane, table, side):
    def lines(dz):
        below = source[table[0][dz], plane, side - 1 : side]
        centre = source[table[1][dz], plane]
        above = source[table[2][dz], plane, 0:1]
        return jnp.concatenate([below, centre, above], axis=0)

    left, centre, right = lines(0), lines(1), lines(2)
    at = lax.broadcasted_iota(jnp.int32, centre.shape, 1)
    ahead = pltpu.roll(jnp.where(at == 0, right, centre), side - 1, 1)
    behind = pltpu.roll(jnp.where(at == side - 1, left, centre), 1, 1)
    for oy in range(3):
        for oz, values in enumerate((ahead, centre, behind)):
            column = (oy * 3 + oz) * LANES
            part = values[2 - oy : 2 - oy + side].reshape(side * side, LANES)
            unrolled[row : row + side * side, column : column + LANES] = part.astype(bf16)


def inner_kernel(side, counts, neighbors, acts, preact, cotangent, sums, grads, field, unrolled, turned):
    position = lax.axis_index(AXES)
    slots = acts.shape[0]
    total = slots * counts.shape[0]
    area = side * side
    live = counts[position]
    half = side // 2

    def gate(brick, carry):
        for part in range(2):
            rows = pl.ds(part * half * area, half * area)
            values = gated(preact[brick, rows], cotangent[brick, rows])
            grads[brick, rows] = values
            field[brick, part * half : (part + 1) * half] = values.astype(f32).reshape(half, side, side, LANES)
        return carry

    lax.fori_loop(0, live, gate, 0)
    field[slots] = jnp.zeros(field.shape[1:], f32)
    sums[...] = jnp.zeros(sums.shape, f32)

    def brick_step(brick, carry):
        table = neighbour_slots(neighbors, brick, 1, position, slots, total, live)
        for plane in range(side):
            fill(unrolled, plane * area, field, plane, table, side)
        block = acts[brick]
        none = jnp.zeros((area, LANES), bf16)
        turned[0:LANES] = jnp.concatenate([none, block[:-area]], axis=0).T
        turned[LANES : 2 * LANES] = block.T
        turned[2 * LANES :] = jnp.concatenate([block[area:], none], axis=0).T
        sums[...] += jnp.dot(turned[...], unrolled[...], preferred_element_type=f32)
        return carry

    lax.fori_loop(0, live, brick_step, 0)


def load_edges(field, edge):
    slots = edge.shape[0]
    field[0:slots] = edge[...].astype(f32).reshape(field[0:slots].shape)
    field[slots] = jnp.zeros(field.shape[1:], f32)


def outer_kernel(
    side, rows, half, counts, neighbors, low_acts, high_acts, below, above, sums, mine, other,
    field, unrolled, table_sum,
):
    position = lax.axis_index(AXES)
    rep = lax.axis_index("rep")
    slots = below.shape[0]
    total = slots * counts.shape[0]
    area = side * side
    live = counts[position]
    extra = []
    for layer, edge, block in ((0, below, low_acts), (2, above, high_acts)):
        load_edges(field, edge)
        for brick in range(slots):
            table = neighbour_slots(neighbors, brick, layer, position, slots, total, live)
            fill(unrolled, brick * area, field, 0, table, side)
        flat = block[...].reshape(slots * area, LANES)
        extra.append(jnp.dot(flat.T, unrolled[...], preferred_element_type=f32))
    adds = (extra[1], None, extra[0])
    for ox in range(3):
        for column in range(9):
            part = sums[ox * LANES : (ox + 1) * LANES, column * LANES : (column + 1) * LANES]
            if adds[ox] is not None:
                part = part + adds[ox][:, column * LANES : (column + 1) * LANES]
            start = (ox * 9 + column) * LANES
            table_sum[start : start + LANES] = part
    count = 27 * LANES
    table_sum[count:] = jnp.zeros((table_sum.shape[0] - count, LANES), f32)
    blocks, padded = mine.shape[0], mine.shape[1]
    lane = lax.broadcasted_iota(jnp.int32, (padded, LANES), 1)
    for block in range(blocks):
        top = table_sum[block * rows : block * rows + padded]
        bottom = table_sum[block * rows + half : block * rows + half + padded]
        top_turned, bottom_turned = pltpu.roll(top, LANES // 2, 1), pltpu.roll(bottom, LANES // 2, 1)
        first = jnp.where(lane < LANES // 2, top, bottom_turned)
        second = jnp.where(lane < LANES // 2, top_turned, bottom)
        mine[block] = jnp.where(rep == 0, first, second)
        other[block] = jnp.where(rep == 0, second, first).astype(bf16)


def input_kernel(
    side, rows, half, counts, neighbors, grads, below, above, shards, out,
    field, low_field, high_field, unrolled, wide, filt, product,
):
    position = lax.axis_index(AXES)
    space, rep = lax.axis_index("space"), lax.axis_index("rep")
    slots = grads.shape[0]
    total = slots * counts.shape[0]
    area = side * side
    voxels = area * side
    live = counts[position]
    blocks, padded = shards.shape[1], shards.shape[2]
    lane = lax.broadcasted_iota(jnp.int32, (padded, LANES), 1)
    for block in range(blocks):
        first = shards[rep, block ^ space].astype(f32)
        second = shards[1 - rep, block ^ space].astype(f32)
        top = jnp.where(lane < LANES // 2, first, pltpu.roll(second, LANES // 2, 1))
        bottom = jnp.where(lane < LANES // 2, pltpu.roll(first, LANES // 2, 1), second)
        wide[block * rows : block * rows + half] = top[:half]
        wide[block * rows + half : block * rows + 2 * half] = bottom[:half]
    for ox in range(3):
        for column in range(9):
            start = (ox * 9 + column) * LANES
            block = wide[start : start + LANES].astype(bf16)
            filt[ox * LANES : (ox + 1) * LANES, column * LANES : (column + 1) * LANES] = block

    def widen(brick, carry):
        field[brick] = grads[brick].astype(f32).reshape(field.shape[1:])
        return carry

    lax.fori_loop(0, live, widen, 0)
    field[slots] = jnp.zeros(field.shape[1:], f32)
    load_edges(low_field, below)
    load_edges(high_field, above)

    def brick_step(brick, carry):
        table = neighbour_slots(neighbors, brick, 0, position, slots, total, live)
        fill(unrolled, 0, low_field, 0, table, side)
        table = neighbour_slots(neighbors, brick, 1, position, slots, total, live)
        for plane in range(side):
            fill(unrolled, (plane + 1) * area, field, plane, table, side)
        table = neighbour_slots(neighbors, brick, 2, position, slots, total, live)
        fill(unrolled, (side + 1) * area, high_field, 0, table, side)
        product[...] = lax.dot_general(
            unrolled[...], filt[...], (((1,), (1,)), ((), ())), preferred_element_type=f32
        )
        total_sum = product[2 * area : 2 * area + voxels, 0:LANES]
        total_sum += product[area : area + voxels, LANES : 2 * LANES]
        total_sum += product[0:voxels, 2 * LANES :]
        out[brick] = total_sum.astype(bf16)
        return carry

    lax.fori_loop(0, live, brick_step, 0)

    def clear(brick, carry):
        out[brick] = jnp.zeros((voxels, LANES), bf16)
        return carry

    lax.fori_loop(live, slots, clear, 0)


def call(kernel, outs, specs, scratch, flops):
    whole = pl.BlockSpec(memory_space=pltpu.VMEM)
    scalars = pl.BlockSpec(memory_space=pltpu.SMEM)
    return pl.pallas_call(
        kernel,
        out_shape=outs,
        in_specs=[scalars, scalars] + [whole] * specs,
        out_specs=jax.tree.map(lambda _: whole, outs),
        scratch_shapes=scratch,
        cost_estimate=pl.CostEstimate(flops=flops, bytes_accessed=4 << 20, transcendentals=0),
        compiler_params=pltpu.CompilerParams(vmem_limit_bytes=40 << 20),
    )


def on_device(acts, preact, cotangent, filt, counts, neighbors):
    slots, voxels, channels = acts.shape
    side = round(voxels ** (1 / 3))
    area = side * side
    spaces = lax.axis_size("space")
    devices = lax.axis_size(AXES)
    space = lax.axis_index("space")
    rows = filt.shape[0]
    half = (rows + 1) // 2
    padded = -(-half // 16) * 16
    steps = steps_of(spaces)

    top = filt[:half]
    bottom = jnp.pad(filt[half:], ((0, 2 * half - rows), (0, 0)))
    shards = jnp.pad(jnp.concatenate([top, bottom], axis=1), ((0, padded - half), (0, 0)))[None]
    for unit, members in reversed(steps):
        arrived = [shards] + [swapped(shards, "space", unit * m) for m in range(1, members)]
        shards = jnp.stack(arrived, axis=1).reshape((-1,) + shards.shape[1:])
    shards = jnp.stack([shards, swapped(shards, "rep", 1)])

    high = gated(preact[:, voxels - area :], cotangent[:, voxels - area :])
    low = gated(preact[:, :area], cotangent[:, :area])
    below = shifted(high, 1)
    above = shifted(low, -1)

    field = pltpu.VMEM((slots + 1, side, side, side, channels), f32)
    edges = pltpu.VMEM((slots + 1, 1, side, side, channels), f32)
    sums, grads = call(
        functools.partial(inner_kernel, side),
        (
            jax.ShapeDtypeStruct((3 * channels, 9 * channels), f32),
            jax.ShapeDtypeStruct(acts.shape, bf16),
        ),
        3,
        [
            field,
            pltpu.VMEM((voxels, 9 * channels), bf16),
            pltpu.VMEM((3 * channels, voxels), bf16),
        ],
        10**10,
    )(counts, neighbors, acts, preact, cotangent)
    mine, other = call(
        functools.partial(outer_kernel, side, rows, half),
        (
            jax.ShapeDtypeStruct((spaces, padded, LANES), f32),
            jax.ShapeDtypeStruct((spaces, padded, LANES), bf16),
        ),
        5,
        [
            edges,
            pltpu.VMEM((slots * area, 9 * channels), bf16),
            pltpu.VMEM((27 * channels + 16, channels), f32),
        ],
        10**9,
    )(counts, neighbors, acts[:, :area], acts[:, voxels - area :], below, above, sums)

    input_grad = call(
        functools.partial(input_kernel, side, rows, half),
        jax.ShapeDtypeStruct(acts.shape, bf16),
        4,
        [
            field,
            edges,
            edges,
            pltpu.VMEM((voxels + 2 * area, 9 * channels), bf16),
            pltpu.VMEM((27 * channels + 16, channels), f32),
            pltpu.VMEM((3 * channels, 9 * channels), bf16),
            pltpu.VMEM((voxels + 2 * area, 3 * channels), f32),
        ],
        10**10,
    )(counts, neighbors, grads, below, above, shards)

    held = mine + swapped(other, "rep", 1).astype(f32)
    for unit, members in steps:
        held = held.reshape((-1, members) + held.shape[1:])
        sent = held.astype(bf16)
        own = space // unit % members
        arrived = [
            swapped(lax.dynamic_index_in_dim(sent, own ^ m, 1, False), "space", unit * m)
            for m in range(1, members)
        ]
        held = lax.dynamic_index_in_dim(held, own, 1, False)
        for block in arrived:
            held = held + block.astype(f32)
    held = held[0] * (1.0 / math.sqrt(slots * devices * voxels))
    columns = channels // 2
    filt_grad = jnp.concatenate([held[:half, :columns], held[: rows - half, columns:]], axis=0)
    return input_grad, filt_grad


def solution(mesh):
    in_specs = (
        P(AXES, None, None),
        P(AXES, None, None),
        P(AXES, None, None),
        P("space", "rep"),
        P(),
        P(AXES, None),
    )
    out_specs = (P(AXES, None, None), P("space", "rep"))
    return jax.shard_map(
        on_device, mesh=mesh, in_specs=in_specs, out_specs=out_specs, check_vma=False
    )
```

```python
import functools
import math

import jax
import jax.numpy as jnp
from jax import lax
from jax.experimental import pallas as pl
from jax.experimental.pallas import tpu as pltpu
from jax.sharding import PartitionSpec as P

f32 = jnp.float32
bf16 = jnp.bfloat16
AXES = ("space", "rep")
LANES = 128


def silu_slope(values):
    sigma = jax.nn.sigmoid(values)
    return sigma * (1.0 + values * (1.0 - sigma))


def gated(preact, cotangent):
    return (cotangent.astype(f32) * silu_slope(preact.astype(f32))).astype(bf16)


def with_neighbour(x, first):
    count = lax.axis_size(AXES)
    pairs = []
    for low in range(first, count - 1, 2):
        pairs += [(low, low + 1), (low + 1, low)]
    return lax.ppermute(x, AXES, pairs)


def swapped(x, axis, mask):
    count = lax.axis_size(axis)
    return lax.ppermute(x, axis, [(i, i ^ mask) for i in range(count)])


def steps_of(count):
    out, unit = [], 1
    while unit < count:
        members = min(4, count // unit)
        out.append((unit, members))
        unit *= members
    return out


def neighbour_slots(nb_ref, brick, layer, position, slots, total, live):
    base = (position + (layer - 1)) * slots
    row_of = jnp.minimum(brick, slots - 1)
    table = []
    for dy in range(3):
        row = []
        for dz in range(3):
            value = nb_ref[row_of, layer * 9 + dy * 3 + dz]
            row.append(jnp.where((value >= total) | (brick >= live), slots, value - base))
        table.append(row)
    return table


def fill(unrolled, row, source, plane, table, side):
    def lines(dz):
        below = source[table[0][dz], plane, side - 1 : side]
        centre = source[table[1][dz], plane]
        above = source[table[2][dz], plane, 0:1]
        return jnp.concatenate([below, centre, above], axis=0)

    left, centre, right = lines(0), lines(1), lines(2)
    at = lax.broadcasted_iota(jnp.int32, centre.shape, 1)
    ahead = pltpu.roll(jnp.where(at == 0, right, centre), side - 1, 1)
    behind = pltpu.roll(jnp.where(at == side - 1, left, centre), 1, 1)
    for oy in range(3):
        for oz, values in enumerate((ahead, centre, behind)):
            column = (oy * 3 + oz) * LANES
            part = values[2 - oy : 2 - oy + side].reshape(side * side, LANES)
            unrolled[row : row + side * side, column : column + LANES] = part.astype(bf16)


def fill_brick(unrolled, field, neighbors, brick, live, counts, side, slots):
    position = lax.axis_index(AXES)
    table = neighbour_slots(
        neighbors, brick, 1, position, slots, slots * counts.shape[0], live
    )
    for plane in range(side):
        fill(unrolled, plane * side * side, field, plane, table, side)


def gate_kernel(
    side, counts, preact_far, cotangent_far, grads, near, far, preact, cotangent, sems
):
    live = counts[lax.axis_index(AXES)]
    rep = lax.axis_index("rep")
    area = side * side
    middle = preact.shape[1] // 2
    loads = [loader(preact_far, preact, sems, 0), loader(cotangent_far, cotangent, sems, 1)]
    start_all(0, live, *loads)

    def gate(brick, carry):
        for load in loads:
            load(brick).wait()
        ends = []
        for part in range(2):
            rows = pl.ds(part * middle, middle)
            values = gated(preact[brick, rows], cotangent[brick, rows])
            ends.append(values[:area] if part == 0 else values[-area:])
            grads[brick, rows] = values
        near[brick] = jnp.where(rep == 0, ends[1], ends[0])
        far[brick] = jnp.where(rep == 0, ends[0], ends[1])
        return carry

    lax.fori_loop(0, live, gate, 0)


def filter_step(side, first, live, counts, neighbors, acts, field, sums, unrolled, turned):
    slots = acts.shape[0]
    area = side * side
    sums[...] = jnp.zeros(sums.shape, f32)

    def prepare(brick, turn):
        fill_brick(unrolled[turn], field, neighbors, brick, live, counts, side, slots)
        block = acts[jnp.minimum(brick, live - 1)]
        none = jnp.zeros((area, LANES), bf16)
        turned[turn][0:LANES] = jnp.concatenate([none, block[:-area]], axis=0).T
        turned[turn][LANES : 2 * LANES] = block.T
        turned[turn][2 * LANES :] = jnp.concatenate([block[area:], none], axis=0).T

    def multiply(turn):
        sums[...] += jnp.dot(turned[turn][...], unrolled[turn][...], preferred_element_type=f32)

    @pl.when(live > first)
    def _():
        prepare(first, 0)

        def pair(step, carry):
            brick = first + 2 * step
            prepare(brick + 1, 1)
            multiply(0)
            prepare(brick + 2, 0)
            multiply(1)
            return carry

        lax.fori_loop(0, (live - first + 1) // 2, pair, 0)


def loader(source, target, sems, row):
    def load(brick):
        return pltpu.make_async_copy(source.at[brick], target.at[brick], sems.at[row, brick])

    return load


def start_all(first, last, *loads):
    for load in loads:

        def start(brick, carry, load=load):
            load(brick).start()
            return carry

        lax.fori_loop(first, last, start, 0)


def inner_kernel(
    side, counts, neighbors, acts_far, grads, sums, field, low_acts, high_acts,
    acts, even, odd, even_turned, odd_turned, sems,
):
    live = counts[lax.axis_index(AXES)]
    slots = acts.shape[0]
    area = side * side
    load = loader(acts_far, acts, sems, 0)
    start_all(0, live, load)

    def widen(brick, carry):
        field[brick] = grads[brick].astype(f32).reshape(field.shape[1:])
        return carry

    lax.fori_loop(0, live, widen, 0)
    field[slots] = jnp.zeros(field.shape[1:], f32)

    def wait(brick, carry):
        load(brick).wait()
        return carry

    lax.fori_loop(0, live, wait, 0)
    filter_step(
        side, 0, live, counts, neighbors, acts, field, sums,
        (even, odd), (even_turned, odd_turned),
    )

    def ends(brick, carry):
        low_acts[brick] = acts[brick, :area]
        high_acts[brick] = acts[brick, acts.shape[1] - area :]
        return carry

    def no_ends(brick, carry):
        low_acts[brick] = jnp.zeros(low_acts.shape[1:], bf16)
        high_acts[brick] = jnp.zeros(low_acts.shape[1:], bf16)
        return carry

    lax.fori_loop(0, live, ends, 0)
    lax.fori_loop(live, slots, no_ends, 0)


def outer_kernel(
    side, rows, half, counts, neighbors, low_acts, high_acts, near, far, sums,
    mine, other, low_field, high_field, unrolled, table_sum,
):
    position = lax.axis_index(AXES)
    rep = lax.axis_index("rep")
    slots = near.shape[0]
    total = slots * counts.shape[0]
    area = side * side
    live = counts[position]
    extra = []
    for layer, field, block in ((0, low_field, low_acts), (2, high_field, high_acts)):
        edge = jnp.where(rep == layer // 2, far[...], near[...])
        field[0:slots] = edge.astype(f32).reshape(field[0:slots].shape)
        field[slots] = jnp.zeros(field.shape[1:], f32)
        for brick in range(slots):
            table = neighbour_slots(neighbors, brick, layer, position, slots, total, live)
            fill(unrolled, brick * area, field, 0, table, side)
        flat = block[...].reshape(slots * area, LANES)
        extra.append(jnp.dot(flat.T, unrolled[...], preferred_element_type=f32))
    adds = (extra[1], None, extra[0])
    for ox in range(3):
        for column in range(9):
            tile = (slice(ox * LANES, (ox + 1) * LANES), slice(column * LANES, (column + 1) * LANES))
            part = sums[tile]
            if adds[ox] is not None:
                part = part + adds[ox][:, tile[1]]
            start = (ox * 9 + column) * LANES
            table_sum[start : start + LANES] = part
    count = 27 * LANES
    table_sum[count:] = jnp.zeros((table_sum.shape[0] - count, LANES), f32)
    blocks, padded = mine.shape[0], mine.shape[1]
    lane = lax.broadcasted_iota(jnp.int32, (padded, LANES), 1)
    for block in range(blocks):
        top = table_sum[block * rows : block * rows + padded]
        bottom = table_sum[block * rows + half : block * rows + half + padded]
        top_turned, bottom_turned = pltpu.roll(top, LANES // 2, 1), pltpu.roll(bottom, LANES // 2, 1)
        first = jnp.where(lane < LANES // 2, top, bottom_turned)
        second = jnp.where(lane < LANES // 2, top_turned, bottom)
        mine[block] = jnp.where(rep == 0, first, second)
        other[block] = jnp.where(rep == 0, second, first).astype(bf16)


def reduce_kernel(unit, members, arrivals, held, *refs):
    arrived, keep, sends = refs[:arrivals], refs[-members], refs[-members + 1 :]
    own = lax.rem(lax.div(lax.axis_index("space"), unit), members)
    for block in range(keep.shape[0]):
        for member in range(members):
            at = block * members + (own ^ member)
            value = held[at]
            for ref in arrived:
                value = value + ref[at].astype(f32)
            if member == 0:
                keep[block] = value
            else:
                sends[member - 1][block] = value.astype(bf16)


def stack_kernel(*refs):
    out = refs[-1]
    members = len(refs) - 1
    for member, ref in enumerate(refs[:-1]):
        for block in range(ref.shape[0]):
            out[block * members + member] = ref[block]


def filter_kernel(rows, half, held, arrived, filt, wide):
    space, rep = lax.axis_index("space"), lax.axis_index("rep")
    blocks, padded = held.shape[0], held.shape[1]
    lane = lax.broadcasted_iota(jnp.int32, (padded, LANES), 1)
    for block in range(blocks):
        own, others = held[block ^ space], arrived[block ^ space]
        first = jnp.where(rep == 0, own, others).astype(f32)
        second = jnp.where(rep == 0, others, own).astype(f32)
        top = jnp.where(lane < LANES // 2, first, pltpu.roll(second, LANES // 2, 1))
        bottom = jnp.where(lane < LANES // 2, pltpu.roll(first, LANES // 2, 1), second)
        wide[block * rows : block * rows + half] = top[:half]
        wide[block * rows + half : block * rows + 2 * half] = bottom[:half]
    for ox in range(3):
        for column in range(9):
            start = (ox * 9 + column) * LANES
            block = wide[start : start + LANES].astype(bf16)
            filt[ox * LANES : (ox + 1) * LANES, column * LANES : (column + 1) * LANES] = block


def input_kernel(
    side, first, last, counts, neighbors, field, low_field, high_field, filt, *refs
):
    out, token, staged, even, odd, edge_rows, product, edge_product, sems = refs[-9:]
    token[...] = jnp.zeros(token.shape, f32)
    unrolled = (even, odd)
    position = lax.axis_index(AXES)
    slots = out.shape[0]
    total = slots * counts.shape[0]
    area = side * side
    live = jnp.minimum(counts[position], last)
    members = last - first

    def times(rows, part):
        return lax.dot_general(
            rows, filt[part], (((1,), (1,)), ((), ())), preferred_element_type=f32
        )

    def prepare(brick, turn):
        fill_brick(unrolled[turn], field, neighbors, brick, live, counts, side, slots)

    def copy(member):
        return pltpu.make_async_copy(staged.at[member], out.at[first + member], sems.at[member])

    def finish(brick, turn):
        member = brick - first
        product[...] = times(unrolled[turn][...], slice(None))
        edge = jnp.minimum(member, members - 1)
        low = edge_product[0, edge] + product[0:area, LANES : 2 * LANES]
        low = low + product[area : 2 * area, 0:LANES]
        middle = product[2 * area :, 0:LANES] + product[area:-area, LANES : 2 * LANES]
        middle = middle + product[: -2 * area, 2 * LANES :]
        high = edge_product[1, edge] + product[-area:, LANES : 2 * LANES]
        high = high + product[-2 * area : -area, 2 * LANES :]
        staged[member, :area] = low.astype(bf16)
        staged[member, area:-area] = middle.astype(bf16)
        staged[member, -area:] = high.astype(bf16)

    def begin(member, carry):
        copy(member).start()
        return carry

    pairs = (jnp.maximum(live - first, 0) + 1) // 2
    early = jnp.maximum(pairs - 1, 0) * 2

    @pl.when(live > first)
    def _():
        for side_of, layer, source, ox in ((0, 0, low_field, 2), (1, 2, high_field, 0)):
            for member in range(members):
                table = neighbour_slots(
                    neighbors, first + member, layer, position, slots, total, live
                )
                fill(edge_rows, member * area, source, 0, table, side)
            values = times(edge_rows[...], slice(ox * LANES, (ox + 1) * LANES))
            edge_product[side_of] = values.reshape(members, area, LANES)
        prepare(first, 0)

        def pair(step, carry):
            brick = first + 2 * step

            @pl.when(step > 0)
            def _():
                copy(2 * step - 2).start()
                copy(2 * step - 1).start()

            prepare(brick + 1, 1)
            finish(brick, 0)
            prepare(brick + 2, 0)
            finish(brick + 1, 1)
            return carry

        lax.fori_loop(0, pairs, pair, 0)

    def clear(member, carry):
        staged[member] = jnp.zeros(staged.shape[1:], bf16)
        return carry

    lax.fori_loop(jnp.maximum(live - first, 0), members, clear, 0)
    lax.fori_loop(early, members, begin, 0)

    def wait(member, carry):
        copy(member).wait()
        return carry

    lax.fori_loop(0, members, wait, 0)


def call(kernel, outs, specs, scratch, flops, out_specs=None, aliases=None, limit=24 << 20):
    places = {"s": pltpu.SMEM, "v": pltpu.VMEM, "a": pl.ANY}
    whole = pl.BlockSpec(memory_space=pltpu.VMEM)
    return pl.pallas_call(
        kernel,
        out_shape=outs,
        in_specs=[pl.BlockSpec(memory_space=places[place]) for place in specs],
        out_specs=out_specs or jax.tree.map(lambda _: whole, outs),
        scratch_shapes=scratch,
        input_output_aliases=aliases or {},
        cost_estimate=pl.CostEstimate(flops=flops, bytes_accessed=1 << 20, transcendentals=0),
        compiler_params=pltpu.CompilerParams(vmem_limit_bytes=limit),
    )


def on_device(acts, preact, cotangent, filt, counts, neighbors):
    slots, voxels, channels = acts.shape
    side = round(voxels ** (1 / 3))
    area = side * side
    spaces = lax.axis_size("space")
    devices = lax.axis_size(AXES)
    rows = filt.shape[0]
    half = (rows + 1) // 2
    padded = -(-half // 16) * 16
    steps = steps_of(spaces)
    split = slots // 2
    flops = 2 * 27 * voxels * channels * channels * slots

    def like(shape, kind):
        return jax.ShapeDtypeStruct(shape, kind)

    top = filt[:half]
    bottom = jnp.pad(filt[half:], ((0, 2 * half - rows), (0, 0)))
    shards = jnp.pad(jnp.concatenate([top, bottom], axis=1), ((0, padded - half), (0, 0)))[None]
    for unit, members in reversed(steps):
        arrived = [shards] + [swapped(shards, "space", unit * m) for m in range(1, members)]
        shards = call(
            stack_kernel,
            like((members * shards.shape[0],) + shards.shape[1:], bf16),
            "v" * members,
            [],
            10**6,
        )(*arrived)
    other_shards = swapped(shards, "rep", 1)

    field_shape = like((slots + 1, side, side, side, channels), f32)
    edge_shape = like((slots + 1, 1, side, side, channels), f32)
    sums_shape = like((3 * channels, 9 * channels), f32)
    plane_shape = like((slots, area, channels), bf16)
    buffers = [pltpu.VMEM((voxels, 9 * channels), bf16)] * 2
    turned = [pltpu.VMEM((3 * channels, voxels), bf16)] * 2
    grads, near, far = call(
        functools.partial(gate_kernel, side),
        (like(acts.shape, bf16), plane_shape, plane_shape),
        "saa",
        [pltpu.VMEM(acts.shape, bf16)] * 2 + [pltpu.SemaphoreType.DMA((2, slots))],
        flops // 5,
        limit=52 << 20,
    )(counts, preact, cotangent)
    near, far = with_neighbour(near, 0), with_neighbour(far, 1)
    sums, field, low_acts, high_acts = call(
        functools.partial(inner_kernel, side),
        (sums_shape, field_shape, plane_shape, plane_shape),
        "ssav",
        [pltpu.VMEM(acts.shape, bf16)] + buffers + turned + [pltpu.SemaphoreType.DMA((1, slots))],
        flops,
    )(counts, neighbors, acts, grads)
    mine, other, low_field, high_field = call(
        functools.partial(outer_kernel, side, rows, half),
        (
            like((spaces, padded, LANES), f32),
            like((spaces, padded, LANES), bf16),
            edge_shape,
            edge_shape,
        ),
        "ssvvvvv",
        [
            pltpu.VMEM((slots * area, 9 * channels), bf16),
            pltpu.VMEM((27 * channels + 16, channels), f32),
        ],
        flops // 5,
    )(counts, neighbors, low_acts, high_acts, near, far, sums)
    wide_filt = call(
        functools.partial(filter_kernel, rows, half),
        like((3 * channels, 9 * channels), bf16),
        "vv",
        [pltpu.VMEM((27 * channels + 16, channels), f32)],
        flops // 8,
    )(shards, other_shards)

    def input_part(first, last, so_far, after):
        given = [counts, neighbors, field, low_field, high_field, wide_filt, after]
        places = "ssvvvva"
        if so_far is not None:
            given.append(so_far)
            places += "a"
        members = last - first
        return call(
            functools.partial(input_kernel, side, first, last),
            (like(acts.shape, bf16), like((8, LANES), f32)),
            places,
            [pltpu.VMEM((members + 1, voxels, channels), bf16)]
            + buffers
            + [
                pltpu.VMEM((members * area, 9 * channels), bf16),
                pltpu.VMEM((voxels, 3 * channels), f32),
                pltpu.VMEM((2, members, area, channels), f32),
                pltpu.SemaphoreType.DMA((members,)),
            ],
            flops // 2,
            out_specs=(pl.BlockSpec(memory_space=pl.ANY), pl.BlockSpec(memory_space=pltpu.VMEM)),
            aliases={} if so_far is None else {len(given) - 1: 0},
        )(*given)

    held, arrived, given = mine, [swapped(other, "rep", 1)], []
    input_grad = None
    parts = [(0, split), (split, slots)]
    for number, (unit, members) in enumerate(steps):
        blocks = held.shape[0] // members
        held, *sends = call(
            functools.partial(reduce_kernel, unit, members, len(arrived)),
            (like((blocks, padded, LANES), f32),)
            + (like((blocks, padded, LANES), bf16),) * (members - 1),
            "v" * (1 + len(arrived)) + "a" * len(given),
            [],
            10**6,
        )(held, *arrived, *given)
        arrived = [swapped(block, "space", unit * (m + 1)) for m, block in enumerate(sends)]
        if number < len(parts):
            input_grad, token = input_part(*parts[number], input_grad, sends[0])
            given = [token]
    for part in parts[len(steps) :]:
        input_grad, _ = input_part(*part, input_grad, sends[0])
    held = held[0]
    for block in arrived:
        held = held + block[0].astype(f32)
    held = held * (1.0 / math.sqrt(slots * devices * voxels))
    columns = channels // 2
    filt_grad = jnp.concatenate([held[:half, :columns], held[: rows - half, columns:]], axis=0)
    return input_grad, filt_grad


def solution(mesh):
    in_specs = (
        P(AXES, None, None),
        P(AXES, None, None),
        P(AXES, None, None),
        P("space", "rep"),
        P(),
        P(AXES, None),
    )
    out_specs = (P(AXES, None, None), P("space", "rep"))
    return jax.shard_map(
        on_device, mesh=mesh, in_specs=in_specs, out_specs=out_specs, check_vma=False
    )
```

```python
import functools
import math

import jax
import jax.numpy as jnp
from jax import lax
from jax.experimental import pallas as pl
from jax.experimental.pallas import tpu as pltpu
from jax.sharding import PartitionSpec as P

f32 = jnp.float32
bf16 = jnp.bfloat16
AXES = ("space", "rep")
LANES = 128


def silu_slope(values):
    sigma = jax.nn.sigmoid(values)
    return sigma * (1.0 + values * (1.0 - sigma))


def gated(preact, cotangent):
    return (cotangent.astype(f32) * silu_slope(preact.astype(f32))).astype(bf16)


def with_neighbour(x, first):
    count = lax.axis_size(AXES)
    pairs = []
    for low in range(first, count - 1, 2):
        pairs += [(low, low + 1), (low + 1, low)]
    return lax.ppermute(x, AXES, pairs)


def swapped(x, axis, mask):
    count = lax.axis_size(axis)
    return lax.ppermute(x, axis, [(i, i ^ mask) for i in range(count)])


def steps_of(count, most):
    out, unit = [], 1
    while unit < count:
        members = min(most, count // unit)
        out.append((unit, members))
        unit *= members
    return out


def neighbour_slots(read, brick, layer, position, slots, total, live, offset=0):
    base = (position + (layer - 1)) * slots - offset
    row_of = jnp.clip(brick, 0, slots - 1)
    table = []
    for dy in range(3):
        row = []
        for dz in range(3):
            value = read(row_of, layer * 9 + dy * 3 + dz)
            row.append(jnp.where((value >= total) | (brick >= live), slots, value - base))
        table.append(row)
    return table


def reader(ref):
    return lambda row, tap: ref[row, tap]


def shares(counts):
    position = lax.axis_index(AXES)
    own, partner = counts[position], counts[position ^ 1]
    gives = lax.div(jnp.maximum(own - partner, 0), 2)
    takes = lax.div(jnp.maximum(partner - own, 0), 2)
    return own, partner, gives, takes


def fill(unrolled, row, source, plane, table, side):
    def lines(dz):
        below = source[table[0][dz], plane, side - 1 : side]
        centre = source[table[1][dz], plane]
        above = source[table[2][dz], plane, 0:1]
        return jnp.concatenate([below, centre, above], axis=0)

    left, centre, right = lines(0), lines(1), lines(2)
    at = lax.broadcasted_iota(jnp.int32, centre.shape, 1)
    ahead = pltpu.roll(jnp.where(at == 0, right, centre), side - 1, 1)
    behind = pltpu.roll(jnp.where(at == side - 1, left, centre), 1, 1)
    for oy in range(3):
        for oz, values in enumerate((ahead, centre, behind)):
            column = (oy * 3 + oz) * LANES
            part = values[2 - oy : 2 - oy + side].reshape(side * side, LANES)
            unrolled[row : row + side * side, column : column + LANES] = part.astype(bf16)


def fill_brick(unrolled, field, table, side):
    for plane in range(side):
        fill(unrolled, plane * side * side, field, plane, table, side)


def gate_kernel(
    side, counts_far, acts_far, preact_far, cotangent_far, after, grads, near, far, acts,
    preact, cotangent, sems, counts, counts_sem,
):
    rep = lax.axis_index("rep")
    slots = preact.shape[0]
    area = side * side
    middle = preact.shape[1] // 2
    load_counts = pltpu.make_async_copy(counts_far, counts, counts_sem)
    load_counts.start()
    loads = [loader(preact_far, preact, sems, 0), loader(cotangent_far, cotangent, sems, 1)]

    def load_acts(brick):
        return pltpu.make_async_copy(acts_far.at[brick], acts.at[brick], sems.at[2, brick])


    def start(brick, carry):
        for load in loads:
            load(brick).start()
        return carry

    lax.fori_loop(0, slots, start, 0)
    start_all(0, slots, load_acts)
    load_counts.wait()
    live = counts[lax.axis_index(AXES)]

    def gate(brick, carry):
        for load in loads:
            load(brick).wait()
        ends = []
        for part in range(2):
            rows = pl.ds(part * middle, middle)
            values = gated(preact[brick, rows], cotangent[brick, rows])
            ends.append(values[:area] if part == 0 else values[-area:])
            grads[brick, rows] = values
        near[brick] = jnp.where(rep == 0, ends[1], ends[0])
        far[brick] = jnp.where(rep == 0, ends[0], ends[1])
        return carry

    def wait_unused(brick, carry):
        for load in loads:
            load(brick).wait()
        return carry

    def wait_acts(brick, carry):
        load_acts(brick).wait()
        return carry

    lax.fori_loop(0, live, gate, 0)
    lax.fori_loop(live, slots, wait_unused, 0)
    lax.fori_loop(0, slots, wait_acts, 0)


def filter_step(side, first, last, table_of, acts, field, sums, unrolled, turned):
    area = side * side

    def prepare(brick, turn):
        fill_brick(unrolled[turn], field, table_of(brick), side)
        block = acts[jnp.minimum(brick, last - 1)]
        none = jnp.zeros((area, LANES), bf16)
        turned[turn][0:LANES] = jnp.concatenate([none, block[:-area]], axis=0).T
        turned[turn][LANES : 2 * LANES] = block.T
        turned[turn][2 * LANES :] = jnp.concatenate([block[area:], none], axis=0).T

    def multiply(turn):
        sums[...] += jnp.dot(turned[turn][...], unrolled[turn][...], preferred_element_type=f32)

    @pl.when(last > first)
    def _():
        prepare(first, 0)

        def pair(step, carry):
            brick = first + 2 * step
            prepare(brick + 1, 1)
            multiply(0)
            prepare(brick + 2, 0)
            multiply(1)
            return carry

        lax.fori_loop(0, lax.div(last - first + 1, 2), pair, 0)


def loader(source, target, sems, row):
    def load(brick):
        return pltpu.make_async_copy(source.at[brick], target.at[brick], sems.at[row, brick])

    return load


def start_all(first, last, *loads):
    for load in loads:

        def start(brick, carry, load=load):
            load(brick).start()
            return carry

        lax.fori_loop(first, last, start, 0)


def inner_kernel(
    side, counts, neighbors, other_neighbors, acts, other_acts, grads, other_grads, after,
    sums, field, token, even, odd, even_turned, odd_turned,
):
    token[...] = jnp.zeros(token.shape, f32)
    position = lax.axis_index(AXES)
    slots = neighbors.shape[0]
    total = slots * counts.shape[0]
    own, partner, gives, takes = shares(counts)

    def widen(brick, carry):
        field[brick] = grads[brick].astype(f32).reshape(field.shape[1:])
        return carry

    def widen_other(brick, carry):
        field[slots + 1 + brick] = other_grads[brick].astype(f32).reshape(field.shape[1:])
        return carry

    lax.fori_loop(0, own, widen, 0)
    lax.fori_loop(0, jnp.where(takes > 0, partner, 0), widen_other, 0)
    field[slots] = jnp.zeros(field.shape[1:], f32)
    sums[...] = jnp.zeros(sums.shape, f32)
    scratch = (even, odd), (even_turned, odd_turned)
    keep = own - gives

    def table(brick):
        return neighbour_slots(reader(neighbors), brick, 1, position, slots, total, keep)

    def other_table(brick):
        return neighbour_slots(
            reader(other_neighbors), brick, 1, position ^ 1, slots, total, partner, slots + 1
        )

    filter_step(side, 0, keep, table, acts, field, sums, *scratch)
    filter_step(side, partner - takes, partner, other_table, other_acts, field, sums, *scratch)


def outer_kernel(
    side, rows, half, counts, neighbors, acts, other_grads, far, sums,
    mine, other, low_field, high_field, unrolled, table_sum,
):
    position = lax.axis_index(AXES)
    rep = lax.axis_index("rep")
    slots = far.shape[0]
    total = slots * counts.shape[0]
    area = side * side
    live = counts[position]
    extra = []
    for layer, field, plane in ((0, low_field, 0), (2, high_field, side - 1)):
        start = (side - 1) * area if layer == 0 else 0
        edge = jnp.where(rep == layer // 2, far[...], other_grads[:, start : start + area])
        field[0:slots] = edge.astype(f32).reshape(field[0:slots].shape)
        field[slots] = jnp.zeros(field.shape[1:], f32)
        for brick in range(slots):
            table = neighbour_slots(reader(neighbors), brick, layer, position, slots, total, live)
            fill(unrolled, brick * area, field, 0, table, side)
        flat = acts[:, plane * area : (plane + 1) * area].reshape(slots * area, LANES)
        extra.append(jnp.dot(flat.T, unrolled[...], preferred_element_type=f32))
    adds = (extra[1], None, extra[0])
    for ox in range(3):
        for column in range(9):
            tile = (slice(ox * LANES, (ox + 1) * LANES), slice(column * LANES, (column + 1) * LANES))
            part = sums[tile]
            if adds[ox] is not None:
                part = part + adds[ox][:, tile[1]]
            start = (ox * 9 + column) * LANES
            table_sum[start : start + LANES] = part
    count = 27 * LANES
    table_sum[count:] = jnp.zeros((table_sum.shape[0] - count, LANES), f32)
    blocks, padded = mine.shape[0], mine.shape[1]
    lane = lax.broadcasted_iota(jnp.int32, (padded, LANES), 1)
    for block in range(blocks):
        top = table_sum[block * rows : block * rows + padded]
        bottom = table_sum[block * rows + half : block * rows + half + padded]
        top_turned, bottom_turned = pltpu.roll(top, LANES // 2, 1), pltpu.roll(bottom, LANES // 2, 1)
        first = jnp.where(lane < LANES // 2, top, bottom_turned)
        second = jnp.where(lane < LANES // 2, top_turned, bottom)
        mine[block] = jnp.where(rep == 0, first, second)
        other[block] = jnp.where(rep == 0, second, first).astype(bf16)


def reduce_kernel(unit, members, arrivals, passes, waits, held, *refs):
    arrived, refs = refs[:arrivals], refs[arrivals + passes + waits :]
    keep, sends = refs[0], refs[1:members]
    own = lax.rem(lax.div(lax.axis_index("space"), unit), members)
    for block in range(keep.shape[0]):
        for member in range(members):
            at = block * members + (own ^ member)
            value = held[at]
            for ref in arrived:
                value = value + ref[at].astype(f32)
            if member == 0:
                keep[block] = value
            else:
                sends[member - 1][block] = value.astype(bf16)


def stack_kernel(members, others, *refs):
    out = refs[members + others]
    for member, ref in enumerate(refs[:members]):
        for block in range(ref.shape[0]):
            out[block * members + member] = ref[block]


def last_kernel(scale, half, arrivals, held, *refs):
    arrived, out = refs[:arrivals], refs[-1]
    value = held[0]
    for ref in arrived:
        value = value + ref[0].astype(f32)
    turned = (value * scale).T
    columns, rows = out.shape
    out[:, :half] = turned[:columns, :half]
    out[:, half:] = turned[columns:, : rows - half]


def filter_kernel(rows, half, held, arrived, filt, wide):
    space, rep = lax.axis_index("space"), lax.axis_index("rep")
    blocks, padded = held.shape[0], held.shape[1]
    lane = lax.broadcasted_iota(jnp.int32, (padded, LANES), 1)
    for block in range(blocks):
        own, others = held[block ^ space], arrived[block ^ space]
        first = jnp.where(rep == 0, own, others).astype(f32)
        second = jnp.where(rep == 0, others, own).astype(f32)
        top = jnp.where(lane < LANES // 2, first, pltpu.roll(second, LANES // 2, 1))
        bottom = jnp.where(lane < LANES // 2, pltpu.roll(first, LANES // 2, 1), second)
        wide[block * rows : block * rows + half] = top[:half]
        wide[block * rows + half : block * rows + 2 * half] = bottom[:half]
    for ox in range(3):
        for column in range(9):
            start = (ox * 9 + column) * LANES
            block = wide[start : start + LANES].astype(bf16)
            filt[ox * LANES : (ox + 1) * LANES, column * LANES : (column + 1) * LANES] = block


def input_step(side, first, last, table_of, field, low, high, filt, staged, scratch, at_step):
    even, odd, edge_rows, product, edge_product = scratch
    unrolled = (even, odd)
    area = side * side
    group = edge_rows.shape[0] // area

    def times(rows, part):
        return lax.dot_general(
            rows, filt[part], (((1,), (1,)), ((), ())), preferred_element_type=f32
        )

    def edges(step, carry):
        for end, layer, source, ox in ((0, 0, low, 2), (1, 2, high, 0)):
            for member in range(group):
                table = table_of(first + step * group + member, layer)
                fill(edge_rows, member * area, source, 0, table, side)
            values = times(edge_rows[...], slice(ox * LANES, (ox + 1) * LANES))
            edge_product[end, pl.ds(step * group, group)] = values.reshape(group, area, LANES)
        return carry

    def prepare(brick, turn):
        fill_brick(unrolled[turn], field, table_of(brick, 1), side)

    def finish(brick, turn):
        member = brick - first
        product[...] = times(unrolled[turn][...], slice(None))
        values = edge_product[0, member] + product[0:area, LANES : 2 * LANES]
        values = values + product[area : 2 * area, 0:LANES]
        staged[member, :area] = values.astype(bf16)
        values = product[2 * area :, 0:LANES] + product[area:-area, LANES : 2 * LANES]
        values = values + product[: -2 * area, 2 * LANES :]
        staged[member, area:-area] = values.astype(bf16)
        values = edge_product[1, member] + product[-area:, LANES : 2 * LANES]
        values = values + product[-2 * area : -area, 2 * LANES :]
        staged[member, -area:] = values.astype(bf16)

    @pl.when(last > first)
    def _():
        lax.fori_loop(0, lax.div(last - first + group - 1, group), edges, 0)
        prepare(first, 0)

        def pair(step, carry):
            brick = first + 2 * step
            at_step(step)
            prepare(brick + 1, 1)
            finish(brick, 0)
            prepare(brick + 2, 0)
            finish(brick + 1, 1)
            return carry

        lax.fori_loop(0, lax.div(last - first + 1, 2), pair, 0)


def loop(first, last, do):
    def body(index, carry):
        do(index)
        return carry

    lax.fori_loop(first, last, body, 0)


def sent_early(first, last):
    return jnp.maximum(lax.div(jnp.maximum(last - first, 0) + 1, 2) - 1, 0) * 2


def input_first_kernel(
    side, counts, neighbors, other_neighbors, field, low, high, near, other_far, filt, after,
    out, give, token, edge_low, edge_high, even, odd, edge_rows, product, edge_product, sems,
):
    token[...] = jnp.zeros(token.shape, f32)
    position = lax.axis_index(AXES)
    rep = lax.axis_index("rep")
    slots = out.shape[0]
    total = slots * counts.shape[0]
    own, partner, gives, takes = shares(counts)
    taking = takes > 0
    first = jnp.where(taking, partner - takes, 0)
    last = jnp.where(taking, partner, lax.div(own - gives + 1, 2))
    offset = jnp.where(taking, slots + 1, 0)
    whose = jnp.where(taking, position ^ 1, position)

    def read(row, tap):
        return jnp.where(taking, other_neighbors[row, tap], neighbors[row, tap])

    def table_of(brick, layer):
        shift = offset if layer == 1 else 0
        return neighbour_slots(read, brick, layer, whose, slots, total, last, shift)

    near_wide = near[...].astype(f32).reshape(low[0:slots].shape)
    far_wide = other_far[...].astype(f32).reshape(low[0:slots].shape)
    edge_low[0:slots] = jnp.where(
        taking, jnp.where(rep == 0, near_wide, far_wide), low[0:slots]
    )
    edge_high[0:slots] = jnp.where(
        taking, jnp.where(rep == 0, far_wide, near_wide), high[0:slots]
    )
    for edge in (edge_low, edge_high):
        edge[slots] = jnp.zeros(edge.shape[1:], f32)

    def copy(brick):
        return pltpu.make_async_copy(give.at[brick], out.at[brick], sems.at[brick])

    def at_step(step):
        @pl.when((step > 0) & jnp.logical_not(taking))
        def _():
            copy(2 * step - 2).start()
            copy(2 * step - 1).start()

    scratch = even, odd, edge_rows, product, edge_product
    input_step(
        side, first, last, table_of, field, edge_low, edge_high, filt, give, scratch, at_step
    )
    mine = jnp.where(taking, 0, last)
    loop(jnp.where(taking, 0, sent_early(first, last)), mine, lambda brick: copy(brick).start())
    loop(0, mine, lambda brick: copy(brick).wait())


def input_rest_kernel(
    side, counts, neighbors, field, low, high, filt, returned, after, so_far,
    out, token, staged, none, even, odd, edge_rows, product, edge_product, sems,
):
    token[...] = jnp.zeros(token.shape, f32)
    position = lax.axis_index(AXES)
    slots = out.shape[0]
    total = slots * counts.shape[0]
    own, partner, gives, takes = shares(counts)
    keep = own - gives
    first = jnp.where(takes > 0, 0, lax.div(keep + 1, 2))
    none[...] = jnp.zeros(none.shape, bf16)

    def table_of(brick, layer):
        return neighbour_slots(reader(neighbors), brick, layer, position, slots, total, keep)

    def copy(source, brick):
        return pltpu.make_async_copy(source, out.at[brick], sems.at[brick])

    loop(keep, own, lambda brick: copy(returned.at[brick - keep], brick).start())
    loop(own, slots, lambda brick: copy(none, brick).start())

    def send(member):
        copy(staged.at[member], first + member).start()

    def at_step(step):
        @pl.when(step > 0)
        def _():
            send(2 * step - 2)
            send(2 * step - 1)

    scratch = even, odd, edge_rows, product, edge_product
    input_step(side, first, keep, table_of, field, low, high, filt, staged, scratch, at_step)
    loop(sent_early(first, keep), keep - first, send)
    loop(first, slots, lambda brick: copy(none, brick).wait())


def call(kernel, outs, specs, scratch, flops, out_specs=None, aliases=None, limit=24 << 20):
    places = {"s": pltpu.SMEM, "v": pltpu.VMEM, "a": pl.ANY}
    whole = pl.BlockSpec(memory_space=pltpu.VMEM)
    return pl.pallas_call(
        kernel,
        out_shape=outs,
        in_specs=[pl.BlockSpec(memory_space=places[place]) for place in specs],
        out_specs=out_specs or jax.tree.map(lambda _: whole, outs),
        scratch_shapes=scratch,
        input_output_aliases=aliases or {},
        cost_estimate=pl.CostEstimate(flops=flops, bytes_accessed=1 << 20, transcendentals=0),
        compiler_params=pltpu.CompilerParams(vmem_limit_bytes=limit),
    )


def on_device(acts, preact, cotangent, filt, counts, neighbors):
    slots, voxels, channels = acts.shape
    side = round(voxels ** (1 / 3))
    area = side * side
    spaces = lax.axis_size("space")
    devices = lax.axis_size(AXES)
    rows = filt.shape[0]
    half = (rows + 1) // 2
    padded = -(-half // 16) * 16
    steps = steps_of(spaces, 4)
    flops = 2 * 27 * voxels * channels * channels * slots

    def like(shape, kind):
        return jax.ShapeDtypeStruct(shape, kind)

    top = filt[:half]
    bottom = jnp.pad(filt[half:], ((0, 2 * half - rows), (0, 0)))
    shards = jnp.pad(jnp.concatenate([top, bottom], axis=1), ((0, padded - half), (0, 0)))[None]
    low = min(4, spaces)
    gather = [(low * unit, members) for unit, members in reversed(steps_of(spaces // low, 2))]
    gather.append((1, low))

    def gather_start(number, own):
        unit, members = gather[number]
        return [own] + [swapped(own, "space", unit * m) for m in range(1, members)]

    def gather_finish(arrived, after=(), passed=()):
        own = arrived[0]
        members = len(arrived)
        waits = len(after) + len(passed)
        whole, anywhere = (pl.BlockSpec(memory_space=place) for place in (pltpu.VMEM, pl.ANY))
        return call(
            functools.partial(stack_kernel, members, waits),
            (like((members * own.shape[0],) + own.shape[1:], bf16),)
            + tuple(like(x.shape, x.dtype) for x in passed),
            "v" * members + "a" * waits,
            [],
            10**6,
            out_specs=(whole,) + (anywhere,) * len(passed),
            aliases={members + len(after) + i: 1 + i for i in range(len(passed))},
        )(*arrived, *after, *passed)

    field_shape = like((2 * slots + 1, side, side, side, channels), f32)
    edge_shape = like((slots + 1, 1, side, side, channels), f32)
    sums_shape = like((3 * channels, 9 * channels), f32)
    plane_shape = like((slots, area, channels), bf16)
    buffers = [pltpu.VMEM((voxels, 9 * channels), bf16)] * 2
    turned = [pltpu.VMEM((3 * channels, voxels), bf16)] * 2
    on_the_way = gather_start(0, shards)
    other_neighbors = swapped(neighbors, "rep", 1)
    grads, near, far, acts = call(
        functools.partial(gate_kernel, side),
        (like(acts.shape, bf16), plane_shape, plane_shape, like(acts.shape, bf16)),
        "aaaaa",
        [pltpu.VMEM(acts.shape, bf16)] * 2
        + [
            pltpu.SemaphoreType.DMA((3, slots)),
            pltpu.SMEM(counts.shape, jnp.int32),
            pltpu.SemaphoreType.DMA,
        ],
        flops // 5,
        limit=50 << 20,
    )(counts, acts, preact, cotangent, shards)
    shards, grads, acts, far = gather_finish(on_the_way, passed=(grads, acts, far))
    other_grads, other_acts = swapped(grads, "rep", 1), swapped(acts, "rep", 1)
    far = with_neighbour(far, 1)
    for number in range(1, len(gather) - 1):
        (shards,) = gather_finish(gather_start(number, shards))
    on_the_way = gather_start(len(gather) - 1, shards)
    sums, field, token = call(
        functools.partial(inner_kernel, side),
        (sums_shape, field_shape, like((8, LANES), f32)),
        "sssvvvva",
        buffers + turned,
        flops,
    )(counts, neighbors, other_neighbors, acts, other_acts, grads, other_grads, shards)
    other_far = swapped(far, "rep", 1)
    (shards,) = gather_finish(on_the_way, (token,))
    other_shards = swapped(shards, "rep", 1)
    mine, other, low_field, high_field = call(
        functools.partial(outer_kernel, side, rows, half),
        (
            like((spaces, padded, LANES), f32),
            like((spaces, padded, LANES), bf16),
            edge_shape,
            edge_shape,
        ),
        "ssvvvv",
        [
            pltpu.VMEM((slots * area, 9 * channels), bf16),
            pltpu.VMEM((27 * channels + 16, channels), f32),
        ],
        flops // 5,
    )(counts, neighbors, acts, other_grads, far, sums)
    wide_filt = call(
        functools.partial(filter_kernel, rows, half),
        like((3 * channels, 9 * channels), bf16),
        "vv",
        [pltpu.VMEM((27 * channels + 16, channels), f32)],
        flops // 8,
    )(shards, other_shards)

    most = (slots + 3) // 4 * 2
    group = 4
    any_place, vector_place = (pl.BlockSpec(memory_space=place) for place in (pl.ANY, pltpu.VMEM))
    scratch = buffers + [
        pltpu.VMEM((group * area, 9 * channels), bf16),
        pltpu.VMEM((voxels, 3 * channels), f32),
        pltpu.VMEM((2, -(-slots // group) * group, area, channels), f32),
        pltpu.SemaphoreType.DMA((slots,)),
    ]
    edge_buffer = pltpu.VMEM(edge_shape.shape, f32)
    token_shape = like((8, LANES), f32)

    def input_first(after):
        return call(
            functools.partial(input_first_kernel, side),
            (like(acts.shape, bf16), like((most, voxels, channels), bf16), token_shape),
            "sssvvvvvva",
            [edge_buffer] * 2 + scratch,
            flops // 2,
            out_specs=(any_place, vector_place, vector_place),
        )(
            counts, neighbors, other_neighbors, field, low_field, high_field, near, other_far,
            wide_filt, after,
        )

    def input_rest(returned, after, so_far):
        return call(
            functools.partial(input_rest_kernel, side),
            (like(acts.shape, bf16), token_shape),
            "ssvvvvvaa",
            [pltpu.VMEM((slots + 1, voxels, channels), bf16), pltpu.VMEM((voxels, channels), bf16)]
            + scratch,
            flops // 2,
            out_specs=(any_place, vector_place),
            aliases={8: 0},
        )(counts, neighbors, field, low_field, high_field, wide_filt, returned, after, so_far)

    held, arrived = mine, [swapped(other, "rep", 1)]
    passed, waits = [], []
    for number, (unit, members) in enumerate(steps):
        blocks = held.shape[0] // members
        inputs = [held, *arrived, *passed, *waits]
        outs = call(
            functools.partial(
                reduce_kernel, unit, members, len(arrived), len(passed), len(waits)
            ),
            (like((blocks, padded, LANES), f32),)
            + (like((blocks, padded, LANES), bf16),) * (members - 1)
            + tuple(like(x.shape, x.dtype) for x in passed),
            "v" * (1 + len(arrived)) + "a" * (len(passed) + len(waits)),
            [],
            10**6,
            out_specs=(vector_place,) * members + (any_place,) * len(passed),
            aliases={1 + len(arrived) + i: members + i for i in range(len(passed))},
        )(*inputs)
        held, sends, passed = outs[0], outs[1:members], outs[members:]
        arrived = [swapped(block, "space", unit * (m + 1)) for m, block in enumerate(sends)]
        if number == 0:
            input_grad, give, token = input_first(sends[0])
            passed, waits = [give], [token]
        if number == 1:
            returned = swapped(passed[0], "rep", 1)
            input_grad, token = input_rest(returned, sends[0], input_grad)
            passed, waits = [], [token]
    filt_grad = call(
        functools.partial(last_kernel, 1.0 / math.sqrt(slots * devices * voxels), half, len(arrived)),
        like(filt.shape[::-1], f32),
        "v" * (1 + len(arrived)) + "a" * len(waits),
        [],
        10**6,
    )(held, *arrived, *waits)
    return input_grad, filt_grad.T


def solution(mesh):
    in_specs = (
        P(AXES, None, None),
        P(AXES, None, None),
        P(AXES, None, None),
        P("space", "rep"),
        P(),
        P(AXES, None),
    )
    out_specs = (P(AXES, None, None), P("space", "rep"))
    return jax.shard_map(
        on_device, mesh=mesh, in_specs=in_specs, out_specs=out_specs, check_vma=False
    )
```

```python
import functools
import math

import jax
import jax.numpy as jnp
from jax import lax
from jax.experimental import pallas as pl
from jax.experimental.pallas import tpu as pltpu
from jax.sharding import PartitionSpec as P

f32 = jnp.float32
bf16 = jnp.bfloat16
AXES = ("space", "rep")
LANES = 128


def silu_slope(values):
    sigma = jax.nn.sigmoid(values)
    return sigma * (1.0 + values * (1.0 - sigma))


def gated(preact, cotangent):
    return (cotangent.astype(f32) * silu_slope(preact.astype(f32))).astype(bf16)


def with_neighbour(x, first):
    count = lax.axis_size(AXES)
    pairs = []
    for low in range(first, count - 1, 2):
        pairs += [(low, low + 1), (low + 1, low)]
    return lax.ppermute(x, AXES, pairs)


def swapped(x, axis, mask):
    count = lax.axis_size(axis)
    return lax.ppermute(x, axis, [(i, i ^ mask) for i in range(count)])


def steps_of(count, most):
    out, unit = [], 1
    while unit < count:
        members = min(most, count // unit)
        out.append((unit, members))
        unit *= members
    return out


def loop(first, last, do):
    def body(index, carry):
        do(index)
        return carry

    lax.fori_loop(first, last, body, 0)


def neighbour_slots(read, brick, layer, position, slots, total, live, offset=0):
    base = (position + (layer - 1)) * slots - offset
    row_of = jnp.clip(brick, 0, slots - 1)
    table = []
    for dy in range(3):
        row = []
        for dz in range(3):
            value = read(row_of, layer * 9 + dy * 3 + dz)
            row.append(jnp.where((value >= total) | (brick >= live), slots, value - base))
        table.append(row)
    return table


def reader(ref):
    return lambda row, tap: ref[row, tap]


def shares(counts, slots):
    position = lax.axis_index(AXES)
    own, partner = counts[position], counts[position ^ 1]
    most = slots // 3
    gives = jnp.minimum(lax.div(jnp.maximum(own - partner, 0), 2), most)
    takes = jnp.minimum(lax.div(jnp.maximum(partner - own, 0), 2), most)
    return own, partner, gives, takes


def first_share(keep, takes):
    return jnp.maximum(2 * lax.div(keep + takes + 3, 4), takes)


def fill(unrolled, row, source, plane, table, side):
    def lines(dz):
        below = source[table[0][dz], plane, side - 1 : side]
        centre = source[table[1][dz], plane]
        above = source[table[2][dz], plane, 0:1]
        return jnp.concatenate([below, centre, above], axis=0)

    left, centre, right = lines(0), lines(1), lines(2)
    at = lax.broadcasted_iota(jnp.int32, centre.shape, 1)
    ahead = pltpu.roll(jnp.where(at == 0, right, centre), side - 1, 1)
    behind = pltpu.roll(jnp.where(at == side - 1, left, centre), 1, 1)
    for oy in range(3):
        for oz, values in enumerate((ahead, centre, behind)):
            column = (oy * 3 + oz) * LANES
            part = values[2 - oy : 2 - oy + side].reshape(side * side, LANES)
            unrolled[row : row + side * side, column : column + LANES] = part.astype(bf16)


def fill_brick(unrolled, field, table, side):
    for plane in range(side):
        fill(unrolled, plane * side * side, field, plane, table, side)


def gate_kernel(
    side, acts_far, preact_far, cotangent_far, grads, near, far, acts,
    preact, cotangent, sems,
):
    rep = lax.axis_index("rep")
    slots = preact.shape[0]
    area = side * side
    middle = preact.shape[1] // 2
    loads = [loader(preact_far, preact, sems, 0), loader(cotangent_far, cotangent, sems, 1)]
    load_acts = loader(acts_far, acts, sems, 2)

    def start(brick):
        for load in loads:
            load(brick).start()

    loop(0, slots, start)
    loop(0, slots, lambda brick: load_acts(brick).start())

    def gate(brick):
        for load in loads:
            load(brick).wait()
        ends = []
        for part in range(2):
            rows = pl.ds(part * middle, middle)
            values = gated(preact[brick, rows], cotangent[brick, rows])
            ends.append(values[:area] if part == 0 else values[-area:])
            grads[brick, rows] = values
        near[brick] = jnp.where(rep == 0, ends[1], ends[0])
        far[brick] = jnp.where(rep == 0, ends[0], ends[1])

    loop(0, slots, gate)
    loop(0, slots, lambda brick: load_acts(brick).wait())


def filter_step(side, first, last, table_of, acts, field, sums, unrolled, turned):
    area = side * side

    def prepare(brick, turn):
        fill_brick(unrolled[turn], field, table_of(brick), side)
        block = acts[jnp.minimum(brick, last - 1)]
        none = jnp.zeros((area, LANES), bf16)
        turned[turn][0:LANES] = jnp.concatenate([none, block[:-area]], axis=0).T
        turned[turn][LANES : 2 * LANES] = block.T
        turned[turn][2 * LANES :] = jnp.concatenate([block[area:], none], axis=0).T

    def multiply(turn):
        sums[...] += jnp.dot(turned[turn][...], unrolled[turn][...], preferred_element_type=f32)

    @pl.when(last > first)
    def _():
        prepare(first, 0)

        def pair(step, carry):
            brick = first + 2 * step
            prepare(brick + 1, 1)
            multiply(0)
            prepare(brick + 2, 0)
            multiply(1)
            return carry

        lax.fori_loop(0, lax.div(last - first + 1, 2), pair, 0)


def loader(source, target, sems, row):
    def load(brick):
        return pltpu.make_async_copy(source.at[brick], target.at[brick], sems.at[row, brick])

    return load


def inner_kernel(
    side, counts, neighbors, other_neighbors, acts, other_acts, grads, other_grads, after,
    sums, field, token, even, odd, even_turned, odd_turned,
):
    token[...] = jnp.zeros(token.shape, f32)
    position = lax.axis_index(AXES)
    slots = neighbors.shape[0]
    total = slots * counts.shape[0]
    own, partner, gives, takes = shares(counts, slots)

    def widen(brick, carry):
        field[brick] = grads[brick].astype(f32).reshape(field.shape[1:])
        return carry

    def widen_other(brick, carry):
        field[slots + 1 + brick] = other_grads[brick].astype(f32).reshape(field.shape[1:])
        return carry

    lax.fori_loop(0, own, widen, 0)
    lax.fori_loop(0, jnp.where(takes > 0, partner, 0), widen_other, 0)
    field[slots] = jnp.zeros(field.shape[1:], f32)
    sums[...] = jnp.zeros(sums.shape, f32)
    scratch = (even, odd), (even_turned, odd_turned)
    keep = own - gives

    def table(brick):
        return neighbour_slots(reader(neighbors), brick, 1, position, slots, total, keep)

    def other_table(brick):
        return neighbour_slots(
            reader(other_neighbors), brick, 1, position ^ 1, slots, total, partner, slots + 1
        )

    filter_step(side, 0, keep, table, acts, field, sums, *scratch)
    filter_step(side, partner - takes, partner, other_table, other_acts, field, sums, *scratch)


def outer_kernel(
    side, rows, half, counts, neighbors, acts, other_grads, far, sums, after,
    mine, sent, low_field, high_field, unrolled, table_sum,
):
    position = lax.axis_index(AXES)
    rep = lax.axis_index("rep")
    slots = far.shape[0]
    total = slots * counts.shape[0]
    area = side * side
    live = counts[position]
    extra = []
    for layer, field, plane in ((0, low_field, 0), (2, high_field, side - 1)):
        start = (side - 1) * area if layer == 0 else 0
        edge = jnp.where(rep == layer // 2, far[...], other_grads[:, start : start + area])
        field[0:slots] = edge.astype(f32).reshape(field[0:slots].shape)
        field[slots] = jnp.zeros(field.shape[1:], f32)
        for brick in range(slots):
            table = neighbour_slots(reader(neighbors), brick, layer, position, slots, total, live)
            fill(unrolled, brick * area, field, 0, table, side)
        flat = acts[:, plane * area : (plane + 1) * area].reshape(slots * area, LANES)
        extra.append(jnp.dot(flat.T, unrolled[...], preferred_element_type=f32))
    adds = (extra[1], None, extra[0])
    for ox in range(3):
        for column in range(9):
            tile = (slice(ox * LANES, (ox + 1) * LANES), slice(column * LANES, (column + 1) * LANES))
            part = sums[tile]
            if adds[ox] is not None:
                part = part + adds[ox][:, tile[1]]
            start = (ox * 9 + column) * LANES
            table_sum[start : start + LANES] = part
    count = 27 * LANES
    table_sum[count:] = jnp.zeros((table_sum.shape[0] - count, LANES), f32)
    blocks, padded = mine.shape[0], mine.shape[1]
    lane = lax.broadcasted_iota(jnp.int32, (padded, LANES), 1)
    for block in range(blocks):
        top = table_sum[block * rows : block * rows + padded]
        bottom = table_sum[block * rows + half : block * rows + half + padded]
        top_turned, bottom_turned = pltpu.roll(top, LANES // 2, 1), pltpu.roll(bottom, LANES // 2, 1)
        first = jnp.where(lane < LANES // 2, top, bottom_turned)
        second = jnp.where(lane < LANES // 2, top_turned, bottom)
        mine[block] = jnp.where(rep == 0, first, second)
        start = block * padded
        sent[start : start + padded] = jnp.where(rep == 0, second, first).astype(bf16)
    start = blocks * padded
    sent[start : start + slots * area] = far[...].reshape(slots * area, LANES)


def reduce_kernel(unit, members, arrivals, passes, waits, held, *refs):
    arrived, refs = refs[:arrivals], refs[arrivals + passes + waits :]
    keep, sends = refs[0], refs[1:members]
    own = lax.rem(lax.div(lax.axis_index("space"), unit), members)
    for block in range(keep.shape[0]):
        for member in range(members):
            at = block * members + (own ^ member)
            value = held[at]
            for ref in arrived:
                if len(ref.shape) == 3:
                    part = ref[at]
                else:
                    padded = keep.shape[1]
                    part = ref[pl.ds(pl.multiple_of(at * padded, 16), padded)]
                value = value + part.astype(f32)
            if member == 0:
                keep[block] = value
            else:
                sends[member - 1][block] = value.astype(bf16)


def stack_kernel(members, others, *refs):
    out = refs[members + others]
    for member, ref in enumerate(refs[:members]):
        for block in range(ref.shape[0]):
            out[block * members + member] = ref[block]


def last_kernel(scale, half, arrivals, held, *refs):
    arrived, out = refs[:arrivals], refs[-1]
    value = held[0]
    for ref in arrived:
        value = value + ref[0].astype(f32)
    turned = (value * scale).T
    columns, rows = out.shape
    out[:, :half] = turned[:columns, :half]
    out[:, half:] = turned[columns:, : rows - half]


def filter_kernel(held, arrived, after, filt, wide):
    space, rep = lax.axis_index("space"), lax.axis_index("rep")
    blocks, columns, rows = held.shape
    for block in range(blocks):
        own = held[block ^ space].astype(f32)
        others = arrived[block ^ space].astype(f32)
        at = slice(block * rows, (block + 1) * rows)
        wide[:columns, at] = jnp.where(rep == 0, own, others)
        wide[columns:, at] = jnp.where(rep == 0, others, own)
    for ox in range(3):
        for column in range(9):
            at = (ox * 9 + column) * LANES
            block = wide[:, at : at + LANES].astype(bf16)
            filt[column * LANES : (column + 1) * LANES, ox * LANES : (ox + 1) * LANES] = block


def input_step(side, first, last, table_of, field, low, high, filt, staged, scratch, at_step):
    even, odd, product = scratch
    unrolled = (even, odd)
    area = side * side
    voxels = area * side

    def prepare(brick, turn):
        fill(unrolled[turn], 0, low, 0, table_of(brick, 0), side)
        table = table_of(brick, 1)
        for plane in range(side):
            fill(unrolled[turn], (plane + 1) * area, field, plane, table, side)
        fill(unrolled[turn], (side + 1) * area, high, 0, table_of(brick, 2), side)

    def finish(brick, turn):
        product[...] = jnp.dot(unrolled[turn][...], filt[...], preferred_element_type=f32)
        values = product[2 * area :, 0:LANES] + product[area : area + voxels, LANES : 2 * LANES]
        values = values + product[0:voxels, 2 * LANES :]
        staged[brick - first] = values.astype(bf16)

    @pl.when(last > first)
    def _():
        prepare(first, 0)

        def pair(step, carry):
            brick = first + 2 * step
            at_step(step)
            prepare(brick + 1, 1)
            finish(brick, 0)
            prepare(brick + 2, 0)
            finish(brick + 1, 1)
            return carry

        lax.fori_loop(0, lax.div(last - first + 1, 2), pair, 0)


def sent_early(first, last):
    return jnp.maximum(lax.div(jnp.maximum(last - first, 0) + 1, 2) - 1, 0) * 2


def input_first_kernel(
    side, start, counts, neighbors, other_neighbors, field, low, high, near, arrived, filt, after,
    give, token, edge_low, edge_high, even, odd, product,
):
    token[...] = jnp.zeros(token.shape, f32)
    position = lax.axis_index(AXES)
    rep = lax.axis_index("rep")
    slots = near.shape[0]
    total = slots * counts.shape[0]
    own, partner, gives, takes = shares(counts, slots)
    keep = own - gives
    last = jnp.minimum(first_share(keep, takes), keep + takes)

    def table_of(item, layer):
        taken = item < takes
        brick = jnp.where(taken, partner - takes + item, item - takes)
        whose = jnp.where(taken, position ^ 1, position)
        offset = jnp.where(taken, slots + 1, 0)
        live = jnp.where(item < last, slots, 0)

        def read(row, tap):
            return jnp.where(taken, other_neighbors[row, tap], neighbors[row, tap])

        return neighbour_slots(read, brick, layer, whose, slots, total, live, offset)

    near_wide = near[...].astype(f32).reshape(low[0:slots].shape)
    far_rows = arrived[start : start + slots * side * side]
    far_wide = far_rows.astype(f32).reshape(low[0:slots].shape)
    edge_low[0 : slots + 1] = low[...]
    edge_high[0 : slots + 1] = high[...]
    edge_low[slots + 1 :] = jnp.where(rep == 0, near_wide, far_wide)
    edge_high[slots + 1 :] = jnp.where(rep == 0, far_wide, near_wide)
    scratch = even, odd, product
    input_step(
        side, 0, last, table_of, field, edge_low, edge_high, filt, give, scratch, lambda step: None
    )


def input_rest_kernel(
    side, counts, neighbors, field, low, high, filt, done, returned, after,
    out, token, staged, none, even, odd, product, sems,
):
    token[...] = jnp.zeros(token.shape, f32)
    position = lax.axis_index(AXES)
    slots = out.shape[0]
    total = slots * counts.shape[0]
    own, partner, gives, takes = shares(counts, slots)
    keep = own - gives
    first = jnp.minimum(first_share(keep, takes) - takes, keep)
    none[...] = jnp.zeros(none.shape, bf16)

    def table_of(brick, layer):
        return neighbour_slots(reader(neighbors), brick, layer, position, slots, total, keep)

    def copy(source, brick):
        return pltpu.make_async_copy(source, out.at[brick], sems.at[brick])

    loop(0, first, lambda brick: copy(done.at[takes + brick], brick).start())
    loop(keep, own, lambda brick: copy(returned.at[brick - keep], brick).start())
    loop(own, slots, lambda brick: copy(none, brick).start())

    def send(member):
        copy(staged.at[member], first + member).start()

    def at_step(step):
        @pl.when(step > 0)
        def _():
            send(2 * step - 2)
            send(2 * step - 1)

    scratch = even, odd, product
    input_step(side, first, keep, table_of, field, low, high, filt, staged, scratch, at_step)
    loop(sent_early(first, keep), keep - first, send)
    loop(0, slots, lambda brick: copy(none, brick).wait())


def call(kernel, outs, specs, scratch, flops, out_specs=None, aliases=None, limit=24 << 20):
    places = {"s": pltpu.SMEM, "v": pltpu.VMEM, "a": pl.ANY}
    whole = pl.BlockSpec(memory_space=pltpu.VMEM)
    return pl.pallas_call(
        kernel,
        out_shape=outs,
        in_specs=[pl.BlockSpec(memory_space=places[place]) for place in specs],
        out_specs=out_specs or jax.tree.map(lambda _: whole, outs),
        scratch_shapes=scratch,
        input_output_aliases=aliases or {},
        cost_estimate=pl.CostEstimate(flops=flops, bytes_accessed=1 << 20, transcendentals=0),
        compiler_params=pltpu.CompilerParams(vmem_limit_bytes=limit),
    )


def on_device(acts, preact, cotangent, filt, counts, neighbors):
    slots, voxels, channels = acts.shape
    side = round(voxels ** (1 / 3))
    area = side * side
    spaces = lax.axis_size("space")
    devices = lax.axis_size(AXES)
    rows = filt.shape[0]
    half = (rows + 1) // 2
    padded = -(-half // 16) * 16
    steps = steps_of(spaces, 4)
    flops = 2 * 27 * voxels * channels * channels * slots

    def like(shape, kind):
        return jax.ShapeDtypeStruct(shape, kind)

    shards = filt.T[None]
    low = min(4, spaces)
    gather = [(low * unit, members) for unit, members in reversed(steps_of(spaces // low, 2))]
    gather.append((1, low))

    def gather_start(number, own):
        unit, members = gather[number]
        return [own] + [swapped(own, "space", unit * m) for m in range(1, members)]

    def gather_finish(arrived, after=(), passed=()):
        own = arrived[0]
        members = len(arrived)
        waits = len(after) + len(passed)
        whole, anywhere = (pl.BlockSpec(memory_space=place) for place in (pltpu.VMEM, pl.ANY))
        return call(
            functools.partial(stack_kernel, members, waits),
            (like((members * own.shape[0],) + own.shape[1:], bf16),)
            + tuple(like(x.shape, x.dtype) for x in passed),
            "v" * members + "a" * waits,
            [],
            10**6,
            out_specs=(whole,) + (anywhere,) * len(passed),
            aliases={members + len(after) + i: 1 + i for i in range(len(passed))},
        )(*arrived, *after, *passed)

    field_shape = like((2 * slots + 1, side, side, side, channels), f32)
    edge_shape = like((slots + 1, 1, side, side, channels), f32)
    sums_shape = like((3 * channels, 9 * channels), f32)
    plane_shape = like((slots, area, channels), bf16)
    buffers = [pltpu.VMEM((voxels, 9 * channels), bf16)] * 2
    turned = [pltpu.VMEM((3 * channels, voxels), bf16)] * 2
    on_the_way = gather_start(0, shards)
    other_neighbors = swapped(neighbors, "rep", 1)
    grads, near, far, acts = call(
        functools.partial(gate_kernel, side),
        (like(acts.shape, bf16), plane_shape, plane_shape, like(acts.shape, bf16)),
        "aaa",
        [pltpu.VMEM(acts.shape, bf16)] * 2 + [pltpu.SemaphoreType.DMA((3, slots))],
        flops // 5,
        limit=50 << 20,
    )(acts, preact, cotangent)
    shards, grads, acts, far = gather_finish(on_the_way, passed=(grads, acts, far))
    other_grads, other_acts = swapped(grads, "rep", 1), swapped(acts, "rep", 1)
    far = with_neighbour(far, 1)
    for number in range(1, len(gather) - 1):
        (shards,) = gather_finish(gather_start(number, shards))
    on_the_way = gather_start(len(gather) - 1, shards)
    sums, field, token = call(
        functools.partial(inner_kernel, side),
        (sums_shape, field_shape, like((8, LANES), f32)),
        "sssvvvva",
        buffers + turned,
        flops,
    )(counts, neighbors, other_neighbors, acts, other_acts, grads, other_grads, shards)
    other_far = swapped(far, "rep", 1)
    (shards,) = gather_finish(on_the_way, (token,))
    other_shards = swapped(shards, "rep", 1)
    mine, sent, low_field, high_field = call(
        functools.partial(outer_kernel, side, rows, half),
        (
            like((spaces, padded, LANES), f32),
            like((spaces * padded + slots * area, LANES), bf16),
            edge_shape,
            edge_shape,
        ),
        "ssvvvva",
        [
            pltpu.VMEM((slots * area, 9 * channels), bf16),
            pltpu.VMEM((27 * channels + 16, channels), f32),
        ],
        flops // 5,
    )(counts, neighbors, acts, other_grads, far, sums, shards)
    received = swapped(sent, "rep", 1)
    def whole_filter(after):
        return call(
            filter_kernel,
            like((9 * channels, 3 * channels), bf16),
            "vva",
            [pltpu.VMEM((channels, 27 * channels), f32)],
            10**6,
        )(shards, other_shards, after)

    most = (slots + 3) // 4 * 2
    any_place, vector_place = (pl.BlockSpec(memory_space=place) for place in (pl.ANY, pltpu.VMEM))
    scratch = [pltpu.VMEM((voxels + 2 * area, 9 * channels), bf16)] * 2
    scratch += [pltpu.VMEM((voxels + 2 * area, 3 * channels), f32)]
    edge_buffer = pltpu.VMEM((2 * slots + 1,) + edge_shape.shape[1:], f32)
    token_shape = like((8, LANES), f32)

    def input_first(wide_filt, after):
        return call(
            functools.partial(input_first_kernel, side, spaces * padded),
            (like((most, voxels, channels), bf16), token_shape),
            "sssvvvvvva",
            [edge_buffer] * 2 + scratch,
            flops // 2,
        )(
            counts, neighbors, other_neighbors, field, low_field, high_field, near, received,
            wide_filt, after,
        )

    def input_rest(wide_filt, done, returned, after):
        return call(
            functools.partial(input_rest_kernel, side),
            (like(acts.shape, bf16), token_shape),
            "ssvvvvvva",
            [pltpu.VMEM((slots + 1, voxels, channels), bf16), pltpu.VMEM((voxels, channels), bf16)]
            + scratch
            + [pltpu.SemaphoreType.DMA((slots,))],
            flops // 2,
            out_specs=(any_place, vector_place),
        )(counts, neighbors, field, low_field, high_field, wide_filt, done, returned, after)

    held, arrived = mine, [received]
    passed, waits = [], []
    for number, (unit, members) in enumerate(steps):
        blocks = held.shape[0] // members
        inputs = [held, *arrived, *passed, *waits]
        outs = call(
            functools.partial(
                reduce_kernel, unit, members, len(arrived), len(passed), len(waits)
            ),
            (like((blocks, padded, LANES), f32),)
            + (like((blocks, padded, LANES), bf16),) * (members - 1)
            + tuple(like(x.shape, x.dtype) for x in passed),
            "v" * (1 + len(arrived)) + "a" * (len(passed) + len(waits)),
            [],
            10**6,
            out_specs=(vector_place,) * members + (any_place,) * len(passed),
            aliases={1 + len(arrived) + i: members + i for i in range(len(passed))},
        )(*inputs)
        held, sends, passed = outs[0], outs[1:members], outs[members:]
        arrived = [swapped(block, "space", unit * (m + 1)) for m, block in enumerate(sends)]
        if number == 0:
            wide_filt = whole_filter(sends[0])
            give, token = input_first(wide_filt, sends[0])
            passed, waits = [give], [token]
        if number == 1:
            returned = swapped(passed[0], "rep", 1)
            input_grad, token = input_rest(wide_filt, passed[0], returned, sends[0])
            passed, waits = [], [token]
    filt_grad = call(
        functools.partial(last_kernel, 1.0 / math.sqrt(slots * devices * voxels), half, len(arrived)),
        like(filt.shape[::-1], f32),
        "v" * (1 + len(arrived)) + "a" * len(waits),
        [],
        10**6,
    )(held, *arrived, *waits)
    return input_grad, filt_grad.T


def solution(mesh):
    in_specs = (
        P(AXES, None, None),
        P(AXES, None, None),
        P(AXES, None, None),
        P("space", "rep"),
        P(),
        P(AXES, None),
    )
    out_specs = (P(AXES, None, None), P("space", "rep"))
    return jax.shard_map(
        on_device, mesh=mesh, in_specs=in_specs, out_specs=out_specs, check_vma=False
    )
```

```python
import functools
import math

import jax
import jax.numpy as jnp
from jax import lax
from jax.experimental import pallas as pl
from jax.experimental.pallas import tpu as pltpu
from jax.sharding import PartitionSpec as P

f32 = jnp.float32
bf16 = jnp.bfloat16
AXES = ("space", "rep")
LANES = 128


def silu_slope(values):
    sigma = jax.nn.sigmoid(values)
    return sigma * (1.0 + values * (1.0 - sigma))


def gated(preact, cotangent):
    return (cotangent.astype(f32) * silu_slope(preact.astype(f32))).astype(bf16)


def with_neighbour(x, first):
    count = lax.axis_size(AXES)
    pairs = []
    for low in range(first, count - 1, 2):
        pairs += [(low, low + 1), (low + 1, low)]
    return lax.ppermute(x, AXES, pairs)


def swapped(x, axis, mask):
    count = lax.axis_size(axis)
    return lax.ppermute(x, axis, [(i, i ^ mask) for i in range(count)])


def steps_of(count, most):
    out, unit = [], 1
    while unit < count:
        members = min(most, count // unit)
        out.append((unit, members))
        unit *= members
    return out


def loop(first, last, do):
    def body(index, carry):
        do(index)
        return carry

    lax.fori_loop(first, last, body, 0)


def neighbour_slots(read, brick, layer, position, slots, total, live, offset=0):
    base = (position + (layer - 1)) * slots - offset
    row_of = jnp.clip(brick, 0, slots - 1)
    table = []
    for dy in range(3):
        row = []
        for dz in range(3):
            value = read(row_of, layer * 9 + dy * 3 + dz)
            row.append(jnp.where((value >= total) | (brick >= live), slots, value - base))
        table.append(row)
    return table


def reader(ref):
    return lambda row, tap: ref[row, tap]


def shares(counts, slots):
    position = lax.axis_index(AXES)
    own, partner = counts[position], counts[position ^ 1]
    most = slots // 3
    gives = jnp.minimum(lax.div(jnp.maximum(own - partner, 0), 2), most)
    takes = jnp.minimum(lax.div(jnp.maximum(partner - own, 0), 2), most)
    return own, partner, gives, takes


def first_share(keep, takes):
    return jnp.maximum(2 * lax.div(keep + takes + 3, 4), takes)


def fill(unrolled, row, source, plane, table, side):
    def lines(dz):
        below = source[table[0][dz], plane, side - 1 : side]
        centre = source[table[1][dz], plane]
        above = source[table[2][dz], plane, 0:1]
        return jnp.concatenate([below, centre, above], axis=0)

    left, centre, right = lines(0), lines(1), lines(2)
    at = lax.broadcasted_iota(jnp.int32, centre.shape, 1)
    ahead = pltpu.roll(jnp.where(at == 0, right, centre), side - 1, 1)
    behind = pltpu.roll(jnp.where(at == side - 1, left, centre), 1, 1)
    for oy in range(3):
        for oz, values in enumerate((ahead, centre, behind)):
            column = (oy * 3 + oz) * LANES
            part = values[2 - oy : 2 - oy + side].reshape(side * side, LANES)
            unrolled[row : row + side * side, column : column + LANES] = part.astype(bf16)


def fill_brick(unrolled, field, table, side):
    for plane in range(side):
        fill(unrolled, plane * side * side, field, plane, table, side)


def gate_kernel(
    side, acts_far, preact_far, cotangent_far, grads, near, far, acts,
    preact, cotangent, sems,
):
    rep = lax.axis_index("rep")
    slots = preact.shape[0]
    area = side * side
    middle = preact.shape[1] // 2
    loads = [loader(preact_far, preact, sems, 0), loader(cotangent_far, cotangent, sems, 1)]
    load_acts = loader(acts_far, acts, sems, 2)

    def start(brick):
        for load in loads:
            load(brick).start()

    loop(0, slots, start)
    loop(0, slots, lambda brick: load_acts(brick).start())

    def gate(brick):
        for load in loads:
            load(brick).wait()
        ends = []
        for part in range(2):
            rows = pl.ds(part * middle, middle)
            values = gated(preact[brick, rows], cotangent[brick, rows])
            ends.append(values[:area] if part == 0 else values[-area:])
            grads[brick, rows] = values
        near[brick] = jnp.where(rep == 0, ends[1], ends[0])
        far[brick] = jnp.where(rep == 0, ends[0], ends[1])

    loop(0, slots, gate)
    loop(0, slots, lambda brick: load_acts(brick).wait())


def filter_step(side, first, last, table_of, acts, field, sums, unrolled, turned):
    area = side * side

    def prepare(brick, turn):
        fill_brick(unrolled[turn], field, table_of(brick), side)
        block = acts[jnp.minimum(brick, last - 1)]
        none = jnp.zeros((area, LANES), bf16)
        turned[turn][0:LANES] = jnp.concatenate([none, block[:-area]], axis=0).T
        turned[turn][LANES : 2 * LANES] = block.T
        turned[turn][2 * LANES :] = jnp.concatenate([block[area:], none], axis=0).T

    def multiply(turn):
        sums[...] += jnp.dot(turned[turn][...], unrolled[turn][...], preferred_element_type=f32)

    @pl.when(last > first)
    def _():
        prepare(first, 0)

        def pair(step, carry):
            brick = first + 2 * step
            prepare(brick + 1, 1)
            multiply(0)
            prepare(brick + 2, 0)
            multiply(1)
            return carry

        lax.fori_loop(0, lax.div(last - first + 1, 2), pair, 0)


def loader(source, target, sems, row):
    def load(brick):
        return pltpu.make_async_copy(source.at[brick], target.at[brick], sems.at[row, brick])

    return load


def inner_kernel(
    side, counts, neighbors, other_neighbors, acts, other_acts, grads, other_grads, after,
    sums, field, token, even, odd, even_turned, odd_turned,
):
    token[...] = jnp.zeros(token.shape, f32)
    position = lax.axis_index(AXES)
    slots = neighbors.shape[0]
    total = slots * counts.shape[0]
    own, partner, gives, takes = shares(counts, slots)

    def widen(brick, carry):
        field[brick] = grads[brick].astype(f32).reshape(field.shape[1:])
        return carry

    def widen_other(brick, carry):
        field[slots + 1 + brick] = other_grads[brick].astype(f32).reshape(field.shape[1:])
        return carry

    lax.fori_loop(0, own, widen, 0)
    lax.fori_loop(0, jnp.where(takes > 0, partner, 0), widen_other, 0)
    field[slots] = jnp.zeros(field.shape[1:], f32)
    sums[...] = jnp.zeros(sums.shape, f32)
    scratch = (even, odd), (even_turned, odd_turned)
    keep = own - gives

    def table(brick):
        return neighbour_slots(reader(neighbors), brick, 1, position, slots, total, keep)

    def other_table(brick):
        return neighbour_slots(
            reader(other_neighbors), brick, 1, position ^ 1, slots, total, partner, slots + 1
        )

    filter_step(side, 0, keep, table, acts, field, sums, *scratch)
    filter_step(side, partner - takes, partner, other_table, other_acts, field, sums, *scratch)


def outer_kernel(
    side, rows, half, counts, neighbors, acts, other_grads, far, sums, after,
    mine, sent, low_field, high_field, low_rows, high_rows, table_sum,
):
    position = lax.axis_index(AXES)
    rep = lax.axis_index("rep")
    slots = far.shape[0]
    total = slots * counts.shape[0]
    area = side * side
    live = counts[position]
    extra = []
    for layer, field, plane, unrolled in (
        (0, low_field, 0, low_rows),
        (2, high_field, side - 1, high_rows),
    ):
        start = (side - 1) * area if layer == 0 else 0
        edge = jnp.where(rep == layer // 2, far[...], other_grads[:, start : start + area])
        field[0:slots] = edge.astype(f32).reshape(field[0:slots].shape)
        field[slots] = jnp.zeros(field.shape[1:], f32)
        for brick in range(slots):
            table = neighbour_slots(reader(neighbors), brick, layer, position, slots, total, live)
            fill(unrolled, brick * area, field, 0, table, side)
        flat = acts[:, plane * area : (plane + 1) * area].reshape(slots * area, LANES)
        extra.append(jnp.dot(flat.T, unrolled[...], preferred_element_type=f32))
    adds = (extra[1], None, extra[0])
    for ox in range(3):
        for column in range(9):
            tile = (slice(ox * LANES, (ox + 1) * LANES), slice(column * LANES, (column + 1) * LANES))
            part = sums[tile]
            if adds[ox] is not None:
                part = part + adds[ox][:, tile[1]]
            start = (ox * 9 + column) * LANES
            table_sum[start : start + LANES] = part
    count = 27 * LANES
    table_sum[count:] = jnp.zeros((table_sum.shape[0] - count, LANES), f32)
    blocks, padded = mine.shape[0], mine.shape[1]
    lane = lax.broadcasted_iota(jnp.int32, (padded, LANES), 1)
    for block in range(blocks):
        top = table_sum[block * rows : block * rows + padded]
        bottom = table_sum[block * rows + half : block * rows + half + padded]
        top_turned, bottom_turned = pltpu.roll(top, LANES // 2, 1), pltpu.roll(bottom, LANES // 2, 1)
        first = jnp.where(lane < LANES // 2, top, bottom_turned)
        second = jnp.where(lane < LANES // 2, top_turned, bottom)
        mine[block] = jnp.where(rep == 0, first, second)
        start = block * padded
        sent[start : start + padded] = jnp.where(rep == 0, second, first).astype(bf16)
    start = blocks * padded
    sent[start : start + slots * area] = far[...].reshape(slots * area, LANES)


def reduce_kernel(unit, members, arrivals, passes, waits, held, *refs):
    arrived, refs = refs[:arrivals], refs[arrivals + passes + waits :]
    keep, sends = refs[0], refs[1:members]
    own = lax.rem(lax.div(lax.axis_index("space"), unit), members)
    for block in range(keep.shape[0]):
        for member in range(members):
            at = block * members + (own ^ member)
            value = held[at]
            for ref in arrived:
                if len(ref.shape) == 3:
                    part = ref[at]
                else:
                    padded = keep.shape[1]
                    part = ref[pl.ds(pl.multiple_of(at * padded, 16), padded)]
                value = value + part.astype(f32)
            if member == 0:
                keep[block] = value
            else:
                sends[member - 1][block] = value.astype(bf16)


def stack_kernel(members, others, *refs):
    out = refs[members + others]
    for member, ref in enumerate(refs[:members]):
        for block in range(ref.shape[0]):
            out[block * members + member] = ref[block]


def last_kernel(scale, half, arrivals, held, *refs):
    arrived, out = refs[:arrivals], refs[-1]
    value = held[0]
    for ref in arrived:
        value = value + ref[0].astype(f32)
    turned = (value * scale).T
    columns, rows = out.shape
    out[:, :half] = turned[:columns, :half]
    out[:, half:] = turned[columns:, : rows - half]


def filter_kernel(held, arrived, after, filt, wide):
    space, rep = lax.axis_index("space"), lax.axis_index("rep")
    blocks, columns, rows = held.shape
    for block in range(blocks):
        own = held[block ^ space].astype(f32)
        others = arrived[block ^ space].astype(f32)
        at = slice(block * rows, (block + 1) * rows)
        wide[:columns, at] = jnp.where(rep == 0, own, others)
        wide[columns:, at] = jnp.where(rep == 0, others, own)
    for ox in range(3):
        for column in range(9):
            at = (ox * 9 + column) * LANES
            block = wide[:, at : at + LANES].astype(bf16)
            filt[column * LANES : (column + 1) * LANES, ox * LANES : (ox + 1) * LANES] = block


def input_step(side, first, last, table_of, field, low, high, filt, staged, scratch, at_step):
    even, odd, product = scratch
    unrolled = (even, odd)
    area = side * side
    voxels = area * side

    def prepare(brick, turn):
        fill(unrolled[turn], 0, low, 0, table_of(brick, 0), side)
        table = table_of(brick, 1)
        for plane in range(side):
            fill(unrolled[turn], (plane + 1) * area, field, plane, table, side)
        fill(unrolled[turn], (side + 1) * area, high, 0, table_of(brick, 2), side)

    def finish(brick, turn):
        rows = unrolled[turn]
        product[...] = jnp.dot(
            rows[area:], filt[:, : 2 * LANES], preferred_element_type=f32
        )
        values = jnp.dot(rows[:voxels], filt[:, 2 * LANES :], preferred_element_type=f32)
        values = values + product[area:, :LANES]
        values = values + product[:voxels, LANES:]
        staged[brick - first] = values.astype(bf16)

    @pl.when(last > first)
    def _():
        prepare(first, 0)

        def pair(step, carry):
            brick = first + 2 * step
            at_step(step)
            prepare(brick + 1, 1)
            finish(brick, 0)
            prepare(brick + 2, 0)
            finish(brick + 1, 1)
            return carry

        lax.fori_loop(0, lax.div(last - first + 1, 2), pair, 0)


def sent_early(first, last):
    return jnp.maximum(lax.div(jnp.maximum(last - first, 0) + 1, 2) - 1, 0) * 2


def input_first_kernel(
    side, start, counts, neighbors, other_neighbors, field, low, high, near, arrived, filt, after,
    give, token, edge_low, edge_high, even, odd, product,
):
    token[...] = jnp.zeros(token.shape, f32)
    position = lax.axis_index(AXES)
    rep = lax.axis_index("rep")
    slots = near.shape[0]
    total = slots * counts.shape[0]
    own, partner, gives, takes = shares(counts, slots)
    keep = own - gives
    last = jnp.minimum(first_share(keep, takes), keep + takes)

    def table_of(item, layer):
        taken = item < takes
        brick = jnp.where(taken, partner - takes + item, item - takes)
        whose = jnp.where(taken, position ^ 1, position)
        offset = jnp.where(taken, slots + 1, 0)
        live = jnp.where(item < last, slots, 0)

        def read(row, tap):
            return jnp.where(taken, other_neighbors[row, tap], neighbors[row, tap])

        return neighbour_slots(read, brick, layer, whose, slots, total, live, offset)

    near_wide = near[...].astype(f32).reshape(low[0:slots].shape)
    far_rows = arrived[start : start + slots * side * side]
    far_wide = far_rows.astype(f32).reshape(low[0:slots].shape)
    edge_low[0 : slots + 1] = low[...]
    edge_high[0 : slots + 1] = high[...]
    edge_low[slots + 1 :] = jnp.where(rep == 0, near_wide, far_wide)
    edge_high[slots + 1 :] = jnp.where(rep == 0, far_wide, near_wide)
    scratch = even, odd, product
    input_step(
        side, 0, last, table_of, field, edge_low, edge_high, filt, give, scratch, lambda step: None
    )


def input_rest_kernel(
    side, counts, neighbors, field, low, high, filt, done, returned, after,
    out, token, staged, none, even, odd, product, sems,
):
    token[...] = jnp.zeros(token.shape, f32)
    position = lax.axis_index(AXES)
    slots = out.shape[0]
    total = slots * counts.shape[0]
    own, partner, gives, takes = shares(counts, slots)
    keep = own - gives
    first = jnp.minimum(first_share(keep, takes) - takes, keep)
    none[...] = jnp.zeros(none.shape, bf16)

    def table_of(brick, layer):
        return neighbour_slots(reader(neighbors), brick, layer, position, slots, total, keep)

    def copy(source, brick):
        return pltpu.make_async_copy(source, out.at[brick], sems.at[brick])

    loop(0, first, lambda brick: copy(done.at[takes + brick], brick).start())
    loop(keep, own, lambda brick: copy(returned.at[brick - keep], brick).start())
    loop(own, slots, lambda brick: copy(none, brick).start())

    def send(member):
        copy(staged.at[member], first + member).start()

    def at_step(step):
        @pl.when(step > 0)
        def _():
            send(2 * step - 2)
            send(2 * step - 1)

    scratch = even, odd, product
    input_step(side, first, keep, table_of, field, low, high, filt, staged, scratch, at_step)
    loop(sent_early(first, keep), keep - first, send)
    loop(0, slots, lambda brick: copy(none, brick).wait())


def call(kernel, outs, specs, scratch, flops, out_specs=None, aliases=None, limit=24 << 20):
    places = {"s": pltpu.SMEM, "v": pltpu.VMEM, "a": pl.ANY}
    whole = pl.BlockSpec(memory_space=pltpu.VMEM)
    return pl.pallas_call(
        kernel,
        out_shape=outs,
        in_specs=[pl.BlockSpec(memory_space=places[place]) for place in specs],
        out_specs=out_specs or jax.tree.map(lambda _: whole, outs),
        scratch_shapes=scratch,
        input_output_aliases=aliases or {},
        cost_estimate=pl.CostEstimate(flops=flops, bytes_accessed=1 << 20, transcendentals=0),
        compiler_params=pltpu.CompilerParams(vmem_limit_bytes=limit),
    )


def on_device(acts, preact, cotangent, filt, counts, neighbors):
    slots, voxels, channels = acts.shape
    side = round(voxels ** (1 / 3))
    area = side * side
    spaces = lax.axis_size("space")
    devices = lax.axis_size(AXES)
    rows = filt.shape[0]
    half = (rows + 1) // 2
    padded = -(-half // 16) * 16
    steps = steps_of(spaces, 4)
    flops = 2 * 27 * voxels * channels * channels * slots

    def like(shape, kind):
        return jax.ShapeDtypeStruct(shape, kind)

    shards = filt.T[None]
    low = min(4, spaces)
    gather = [(low * unit, members) for unit, members in reversed(steps_of(spaces // low, 2))]
    gather.append((1, low))

    def gather_start(number, own):
        unit, members = gather[number]
        return [own] + [swapped(own, "space", unit * m) for m in range(1, members)]

    def gather_finish(arrived, after=(), passed=()):
        own = arrived[0]
        members = len(arrived)
        waits = len(after) + len(passed)
        whole, anywhere = (pl.BlockSpec(memory_space=place) for place in (pltpu.VMEM, pl.ANY))
        return call(
            functools.partial(stack_kernel, members, waits),
            (like((members * own.shape[0],) + own.shape[1:], bf16),)
            + tuple(like(x.shape, x.dtype) for x in passed),
            "v" * members + "a" * waits,
            [],
            10**6,
            out_specs=(whole,) + (anywhere,) * len(passed),
            aliases={members + len(after) + i: 1 + i for i in range(len(passed))},
        )(*arrived, *after, *passed)

    field_shape = like((2 * slots + 1, side, side, side, channels), f32)
    edge_shape = like((slots + 1, 1, side, side, channels), f32)
    sums_shape = like((3 * channels, 9 * channels), f32)
    plane_shape = like((slots, area, channels), bf16)
    buffers = [pltpu.VMEM((voxels, 9 * channels), bf16)] * 2
    turned = [pltpu.VMEM((3 * channels, voxels), bf16)] * 2
    on_the_way = gather_start(0, shards)
    other_neighbors = swapped(neighbors, "rep", 1)
    grads, near, far, acts = call(
        functools.partial(gate_kernel, side),
        (like(acts.shape, bf16), plane_shape, plane_shape, like(acts.shape, bf16)),
        "aaa",
        [pltpu.VMEM(acts.shape, bf16)] * 2 + [pltpu.SemaphoreType.DMA((3, slots))],
        flops // 5,
        limit=50 << 20,
    )(acts, preact, cotangent)
    shards, grads, acts, far = gather_finish(on_the_way, passed=(grads, acts, far))
    other_grads, other_acts = swapped(grads, "rep", 1), swapped(acts, "rep", 1)
    far = with_neighbour(far, 1)
    for number in range(1, len(gather) - 1):
        (shards,) = gather_finish(gather_start(number, shards))
    on_the_way = gather_start(len(gather) - 1, shards)
    sums, field, token = call(
        functools.partial(inner_kernel, side),
        (sums_shape, field_shape, like((8, LANES), f32)),
        "sssvvvva",
        buffers + turned,
        flops,
    )(counts, neighbors, other_neighbors, acts, other_acts, grads, other_grads, shards)
    other_far = swapped(far, "rep", 1)
    (shards,) = gather_finish(on_the_way, (token,))
    other_shards = swapped(shards, "rep", 1)
    mine, sent, low_field, high_field = call(
        functools.partial(outer_kernel, side, rows, half),
        (
            like((spaces, padded, LANES), f32),
            like((spaces * padded + slots * area, LANES), bf16),
            edge_shape,
            edge_shape,
        ),
        "ssvvvva",
        [
            pltpu.VMEM((slots * area, 9 * channels), bf16),
            pltpu.VMEM((slots * area, 9 * channels), bf16),
            pltpu.VMEM((27 * channels + 16, channels), f32),
        ],
        flops // 5,
    )(counts, neighbors, acts, other_grads, far, sums, shards)
    received = swapped(sent, "rep", 1)
    def whole_filter(after):
        return call(
            filter_kernel,
            like((9 * channels, 3 * channels), bf16),
            "vva",
            [pltpu.VMEM((channels, 27 * channels), f32)],
            10**6,
        )(shards, other_shards, after)

    most = (slots + 3) // 4 * 2
    any_place, vector_place = (pl.BlockSpec(memory_space=place) for place in (pl.ANY, pltpu.VMEM))
    scratch = [pltpu.VMEM((voxels + 2 * area, 9 * channels), bf16)] * 2
    scratch += [pltpu.VMEM((voxels + area, 2 * channels), f32)]
    edge_buffer = pltpu.VMEM((2 * slots + 1,) + edge_shape.shape[1:], f32)
    token_shape = like((8, LANES), f32)

    def input_first(wide_filt, after):
        return call(
            functools.partial(input_first_kernel, side, spaces * padded),
            (like((most, voxels, channels), bf16), token_shape),
            "sssvvvvvva",
            [edge_buffer] * 2 + scratch,
            flops // 2,
        )(
            counts, neighbors, other_neighbors, field, low_field, high_field, near, received,
            wide_filt, after,
        )

    def input_rest(wide_filt, done, returned, after):
        return call(
            functools.partial(input_rest_kernel, side),
            (like(acts.shape, bf16), token_shape),
            "ssvvvvvva",
            [pltpu.VMEM((slots + 1, voxels, channels), bf16), pltpu.VMEM((voxels, channels), bf16)]
            + scratch
            + [pltpu.SemaphoreType.DMA((slots,))],
            flops // 2,
            out_specs=(any_place, vector_place),
        )(counts, neighbors, field, low_field, high_field, wide_filt, done, returned, after)

    held, arrived = mine, [received]
    passed, waits = [], []
    for number, (unit, members) in enumerate(steps):
        blocks = held.shape[0] // members
        inputs = [held, *arrived, *passed, *waits]
        outs = call(
            functools.partial(
                reduce_kernel, unit, members, len(arrived), len(passed), len(waits)
            ),
            (like((blocks, padded, LANES), f32),)
            + (like((blocks, padded, LANES), bf16),) * (members - 1)
            + tuple(like(x.shape, x.dtype) for x in passed),
            "v" * (1 + len(arrived)) + "a" * (len(passed) + len(waits)),
            [],
            10**6,
            out_specs=(vector_place,) * members + (any_place,) * len(passed),
            aliases={1 + len(arrived) + i: members + i for i in range(len(passed))},
        )(*inputs)
        held, sends, passed = outs[0], outs[1:members], outs[members:]
        arrived = [swapped(block, "space", unit * (m + 1)) for m, block in enumerate(sends)]
        if number == 0:
            wide_filt = whole_filter(sends[0])
            give, token = input_first(wide_filt, sends[0])
            passed, waits = [give], [token]
        if number == 1:
            returned = swapped(passed[0], "rep", 1)
            input_grad, token = input_rest(wide_filt, passed[0], returned, sends[0])
            passed, waits = [], [token]
    filt_grad = call(
        functools.partial(last_kernel, 1.0 / math.sqrt(slots * devices * voxels), half, len(arrived)),
        like(filt.shape[::-1], f32),
        "v" * (1 + len(arrived)) + "a" * len(waits),
        [],
        10**6,
    )(held, *arrived, *waits)
    return input_grad, filt_grad.T


def solution(mesh):
    in_specs = (
        P(AXES, None, None),
        P(AXES, None, None),
        P(AXES, None, None),
        P("space", "rep"),
        P(),
        P(AXES, None),
    )
    out_specs = (P(AXES, None, None), P("space", "rep"))
    return jax.shard_map(
        on_device, mesh=mesh, in_specs=in_specs, out_specs=out_specs, check_vma=False
    )
```

```python
import functools
import math

import jax
import jax.numpy as jnp
from jax import lax
from jax.experimental import pallas as pl
from jax.experimental.pallas import tpu as pltpu
from jax.sharding import PartitionSpec as P

f32 = jnp.float32
bf16 = jnp.bfloat16
AXES = ("space", "rep")
LANES = 128


def silu_slope(values):
    sigma = jax.nn.sigmoid(values)
    return sigma * (1.0 + values * (1.0 - sigma))


def gated(preact, cotangent):
    return (cotangent.astype(f32) * silu_slope(preact.astype(f32))).astype(bf16)


def with_neighbour(x, first):
    count = lax.axis_size(AXES)
    pairs = []
    for low in range(first, count - 1, 2):
        pairs += [(low, low + 1), (low + 1, low)]
    return lax.ppermute(x, AXES, pairs)


def swapped(x, axis, mask):
    count = lax.axis_size(axis)
    return lax.ppermute(x, axis, [(i, i ^ mask) for i in range(count)])


def steps_of(count, most):
    out, unit = [], 1
    while unit < count:
        members = min(most, count // unit)
        out.append((unit, members))
        unit *= members
    return out


def loop(first, last, do):
    def body(index, carry):
        do(index)
        return carry

    lax.fori_loop(first, last, body, 0)


def neighbour_slots(read, brick, layer, position, slots, total, live, offset=0):
    base = (position + (layer - 1)) * slots - offset
    row_of = jnp.clip(brick, 0, slots - 1)
    table = []
    for dy in range(3):
        row = []
        for dz in range(3):
            value = read(row_of, layer * 9 + dy * 3 + dz)
            row.append(jnp.where((value >= total) | (brick >= live), slots, value - base))
        table.append(row)
    return table


def reader(ref):
    return lambda row, tap: ref[row, tap]


def shares(counts, slots):
    position = lax.axis_index(AXES)
    own, partner = counts[position], counts[position ^ 1]
    most = slots // 3
    gives = jnp.minimum(lax.div(jnp.maximum(own - partner, 0), 2), most)
    takes = jnp.minimum(lax.div(jnp.maximum(partner - own, 0), 2), most)
    return own, partner, gives, takes


def first_share(keep, takes):
    return jnp.maximum(2 * lax.div(keep + takes + 3, 4), takes)


def fill(unrolled, row, source, plane, table, side):
    def lines(dz):
        below = source[table[0][dz], plane, side - 1 : side]
        centre = source[table[1][dz], plane]
        above = source[table[2][dz], plane, 0:1]
        return jnp.concatenate([below, centre, above], axis=0)

    left, centre, right = lines(0), lines(1), lines(2)
    at = lax.broadcasted_iota(jnp.int32, centre.shape, 1)
    ahead = pltpu.roll(jnp.where(at == 0, right, centre), side - 1, 1)
    behind = pltpu.roll(jnp.where(at == side - 1, left, centre), 1, 1)
    for oy in range(3):
        for oz, values in enumerate((ahead, centre, behind)):
            column = (oy * 3 + oz) * LANES
            part = values[2 - oy : 2 - oy + side].reshape(side * side, LANES)
            unrolled[row : row + side * side, column : column + LANES] = part.astype(bf16)


def fill_brick(unrolled, field, table, side):
    for plane in range(side):
        fill(unrolled, plane * side * side, field, plane, table, side)


def gate_kernel(
    side, acts_far, preact_far, cotangent_far, grads, near, far, acts,
    preact, cotangent, sems,
):
    rep = lax.axis_index("rep")
    slots = preact.shape[0]
    area = side * side
    middle = preact.shape[1] // 2
    loads = [loader(preact_far, preact, sems, 0), loader(cotangent_far, cotangent, sems, 1)]
    load_acts = loader(acts_far, acts, sems, 2)

    def start(brick):
        for load in loads:
            load(brick).start()

    loop(0, slots, start)
    loop(0, slots, lambda brick: load_acts(brick).start())

    def gate(brick):
        for load in loads:
            load(brick).wait()
        ends = []
        for part in range(2):
            rows = pl.ds(part * middle, middle)
            values = gated(preact[brick, rows], cotangent[brick, rows])
            ends.append(values[:area] if part == 0 else values[-area:])
            grads[brick, rows] = values
        near[brick] = jnp.where(rep == 0, ends[1], ends[0])
        far[brick] = jnp.where(rep == 0, ends[0], ends[1])

    loop(0, slots, gate)
    loop(0, slots, lambda brick: load_acts(brick).wait())


def filter_step(side, first, last, table_of, acts, field, sums, unrolled, turned):
    area = side * side

    def prepare(brick, turn):
        fill_brick(unrolled[turn], field, table_of(brick), side)
        block = acts[jnp.minimum(brick, last - 1)]
        none = jnp.zeros((area, LANES), bf16)
        turned[turn][0:LANES] = jnp.concatenate([none, block[:-area]], axis=0).T
        turned[turn][LANES : 2 * LANES] = block.T
        turned[turn][2 * LANES :] = jnp.concatenate([block[area:], none], axis=0).T

    def multiply(turn):
        sums[...] += jnp.dot(turned[turn][...], unrolled[turn][...], preferred_element_type=f32)

    @pl.when(last > first)
    def _():
        prepare(first, 0)

        def pair(step, carry):
            brick = first + 2 * step
            prepare(brick + 1, 1)
            multiply(0)
            prepare(brick + 2, 0)
            multiply(1)
            return carry

        lax.fori_loop(0, lax.div(last - first + 1, 2), pair, 0)


def loader(source, target, sems, row):
    def load(brick):
        return pltpu.make_async_copy(source.at[brick], target.at[brick], sems.at[row, brick])

    return load


def inner_kernel(
    side, counts, neighbors, other_neighbors, acts, other_acts, grads, other_grads, after,
    sums, field, token, even, odd, even_turned, odd_turned,
):
    token[...] = jnp.zeros(token.shape, f32)
    position = lax.axis_index(AXES)
    slots = neighbors.shape[0]
    total = slots * counts.shape[0]
    own, partner, gives, takes = shares(counts, slots)

    def widen(brick, carry):
        field[brick] = grads[brick].astype(f32).reshape(field.shape[1:])
        return carry

    def widen_other(brick, carry):
        field[slots + 1 + brick] = other_grads[brick].astype(f32).reshape(field.shape[1:])
        return carry

    lax.fori_loop(0, own, widen, 0)
    lax.fori_loop(0, jnp.where(takes > 0, partner, 0), widen_other, 0)
    field[slots] = jnp.zeros(field.shape[1:], f32)
    sums[...] = jnp.zeros(sums.shape, f32)
    scratch = (even, odd), (even_turned, odd_turned)
    keep = own - gives

    def table(brick):
        return neighbour_slots(reader(neighbors), brick, 1, position, slots, total, keep)

    def other_table(brick):
        return neighbour_slots(
            reader(other_neighbors), brick, 1, position ^ 1, slots, total, partner, slots + 1
        )

    filter_step(side, 0, keep, table, acts, field, sums, *scratch)
    filter_step(side, partner - takes, partner, other_table, other_acts, field, sums, *scratch)


def outer_kernel(
    side, rows, half, counts, neighbors, acts, other_grads, far, sums, after,
    mine, sent, low_field, high_field, low_rows, high_rows, table_sum,
):
    position = lax.axis_index(AXES)
    rep = lax.axis_index("rep")
    slots = far.shape[0]
    total = slots * counts.shape[0]
    area = side * side
    live = counts[position]
    extra = []
    for layer, field, plane, unrolled in (
        (0, low_field, 0, low_rows),
        (2, high_field, side - 1, high_rows),
    ):
        start = (side - 1) * area if layer == 0 else 0
        edge = jnp.where(rep == layer // 2, far[...], other_grads[:, start : start + area])
        field[0:slots] = edge.astype(f32).reshape(field[0:slots].shape)
        field[slots] = jnp.zeros(field.shape[1:], f32)
        for brick in range(slots):
            table = neighbour_slots(reader(neighbors), brick, layer, position, slots, total, live)
            fill(unrolled, brick * area, field, 0, table, side)
        flat = acts[:, plane * area : (plane + 1) * area].reshape(slots * area, LANES)
        extra.append(jnp.dot(flat.T, unrolled[...], preferred_element_type=f32))
    adds = (extra[1], None, extra[0])
    for ox in range(3):
        for column in range(9):
            tile = (slice(ox * LANES, (ox + 1) * LANES), slice(column * LANES, (column + 1) * LANES))
            part = sums[tile]
            if adds[ox] is not None:
                part = part + adds[ox][:, tile[1]]
            start = (ox * 9 + column) * LANES
            table_sum[start : start + LANES] = part
    count = 27 * LANES
    table_sum[count:] = jnp.zeros((table_sum.shape[0] - count, LANES), f32)
    blocks, padded = mine.shape[0], mine.shape[1]
    lane = lax.broadcasted_iota(jnp.int32, (padded, LANES), 1)
    for block in range(blocks):
        top = table_sum[block * rows : block * rows + padded]
        bottom = table_sum[block * rows + half : block * rows + half + padded]
        top_turned, bottom_turned = pltpu.roll(top, LANES // 2, 1), pltpu.roll(bottom, LANES // 2, 1)
        first = jnp.where(lane < LANES // 2, top, bottom_turned)
        second = jnp.where(lane < LANES // 2, top_turned, bottom)
        mine[block] = jnp.where(rep == 0, first, second)
        start = block * padded
        sent[start : start + padded] = jnp.where(rep == 0, second, first).astype(bf16)
    start = blocks * padded
    sent[start : start + slots * area] = far[...].reshape(slots * area, LANES)


def reduce_kernel(unit, members, arrivals, passes, waits, held, *refs):
    arrived, refs = refs[:arrivals], refs[arrivals + passes + waits :]
    keep, sends = refs[0], refs[1:members]
    own = lax.rem(lax.div(lax.axis_index("space"), unit), members)
    for block in range(keep.shape[0]):
        for member in range(members):
            at = block * members + (own ^ member)
            value = held[at]
            for ref in arrived:
                if len(ref.shape) == 3:
                    part = ref[at]
                else:
                    padded = keep.shape[1]
                    part = ref[pl.ds(pl.multiple_of(at * padded, 16), padded)]
                value = value + part.astype(f32)
            if member == 0:
                keep[block] = value
            else:
                sends[member - 1][block] = value.astype(bf16)


def stack_kernel(members, others, *refs):
    out = refs[members + others]
    for place, ref in enumerate(refs[:members]):
        member = (members - place) % members
        for block in range(ref.shape[0]):
            out[block * members + member] = ref[block]


def last_kernel(scale, half, arrivals, held, *refs):
    arrived, out = refs[:arrivals], refs[-1]
    value = held[0]
    for ref in arrived:
        value = value + ref[0].astype(f32)
    turned = (value * scale).T
    columns, rows = out.shape
    out[:, :half] = turned[:columns, :half]
    out[:, half:] = turned[columns:, : rows - half]


def filter_kernel(held, arrived, after, filt, wide):
    space, rep = lax.axis_index("space"), lax.axis_index("rep")
    blocks, columns, rows = held.shape
    for block in range(blocks):
        own = held[block ^ space].astype(f32)
        others = arrived[block ^ space].astype(f32)
        at = slice(block * rows, (block + 1) * rows)
        wide[:columns, at] = jnp.where(rep == 0, own, others)
        wide[columns:, at] = jnp.where(rep == 0, others, own)
    for ox in range(3):
        for column in range(9):
            at = (ox * 9 + column) * LANES
            block = wide[:, at : at + LANES].astype(bf16)
            filt[column * LANES : (column + 1) * LANES, ox * LANES : (ox + 1) * LANES] = block


def input_step(side, first, last, table_of, field, low, high, filt, staged, scratch, at_step):
    even, odd, product = scratch
    unrolled = (even, odd)
    area = side * side
    voxels = area * side

    def prepare(brick, turn):
        fill(unrolled[turn], 0, low, 0, table_of(brick, 0), side)
        table = table_of(brick, 1)
        for plane in range(side):
            fill(unrolled[turn], (plane + 1) * area, field, plane, table, side)
        fill(unrolled[turn], (side + 1) * area, high, 0, table_of(brick, 2), side)

    def finish(brick, turn):
        rows = unrolled[turn]
        product[...] = jnp.dot(
            rows[area:], filt[:, : 2 * LANES], preferred_element_type=f32
        )
        values = jnp.dot(rows[:voxels], filt[:, 2 * LANES :], preferred_element_type=f32)
        values = values + product[area:, :LANES]
        values = values + product[:voxels, LANES:]
        staged[brick - first] = values.astype(bf16)

    @pl.when(last > first)
    def _():
        prepare(first, 0)

        def pair(step, carry):
            brick = first + 2 * step
            at_step(step)
            prepare(brick + 1, 1)
            finish(brick, 0)
            prepare(brick + 2, 0)
            finish(brick + 1, 1)
            return carry

        lax.fori_loop(0, lax.div(last - first + 1, 2), pair, 0)


def sent_early(first, last):
    return jnp.maximum(lax.div(jnp.maximum(last - first, 0) + 1, 2) - 1, 0) * 2


def input_first_kernel(
    side, start, counts, neighbors, other_neighbors, field, low, high, near, arrived, filt, after,
    give, token, edge_low, edge_high, even, odd, product,
):
    token[...] = jnp.zeros(token.shape, f32)
    position = lax.axis_index(AXES)
    rep = lax.axis_index("rep")
    slots = near.shape[0]
    total = slots * counts.shape[0]
    own, partner, gives, takes = shares(counts, slots)
    keep = own - gives
    last = jnp.minimum(first_share(keep, takes), keep + takes)

    def table_of(item, layer):
        taken = item < takes
        brick = jnp.where(taken, partner - takes + item, item - takes)
        whose = jnp.where(taken, position ^ 1, position)
        offset = jnp.where(taken, slots + 1, 0)
        live = jnp.where(item < last, slots, 0)

        def read(row, tap):
            return jnp.where(taken, other_neighbors[row, tap], neighbors[row, tap])

        return neighbour_slots(read, brick, layer, whose, slots, total, live, offset)

    near_wide = near[...].astype(f32).reshape(low[0:slots].shape)
    far_rows = arrived[start : start + slots * side * side]
    far_wide = far_rows.astype(f32).reshape(low[0:slots].shape)
    edge_low[0 : slots + 1] = low[...]
    edge_high[0 : slots + 1] = high[...]
    edge_low[slots + 1 :] = jnp.where(rep == 0, near_wide, far_wide)
    edge_high[slots + 1 :] = jnp.where(rep == 0, far_wide, near_wide)
    scratch = even, odd, product
    input_step(
        side, 0, last, table_of, field, edge_low, edge_high, filt, give, scratch, lambda step: None
    )


def input_rest_kernel(
    side, counts, neighbors, field, low, high, filt, done, returned, after,
    out, token, staged, none, even, odd, product, sems,
):
    token[...] = jnp.zeros(token.shape, f32)
    position = lax.axis_index(AXES)
    slots = out.shape[0]
    total = slots * counts.shape[0]
    own, partner, gives, takes = shares(counts, slots)
    keep = own - gives
    first = jnp.minimum(first_share(keep, takes) - takes, keep)
    none[...] = jnp.zeros(none.shape, bf16)

    def table_of(brick, layer):
        return neighbour_slots(reader(neighbors), brick, layer, position, slots, total, keep)

    def copy(source, brick):
        return pltpu.make_async_copy(source, out.at[brick], sems.at[brick])

    loop(0, first, lambda brick: copy(done.at[takes + brick], brick).start())
    loop(keep, own, lambda brick: copy(returned.at[brick - keep], brick).start())
    loop(own, slots, lambda brick: copy(none, brick).start())

    def send(member):
        copy(staged.at[member], first + member).start()

    def at_step(step):
        @pl.when(step > 0)
        def _():
            send(2 * step - 2)
            send(2 * step - 1)

    scratch = even, odd, product
    input_step(side, first, keep, table_of, field, low, high, filt, staged, scratch, at_step)
    loop(sent_early(first, keep), keep - first, send)
    loop(0, slots, lambda brick: copy(none, brick).wait())


def call(kernel, outs, specs, scratch, flops, out_specs=None, aliases=None, limit=24 << 20):
    places = {"s": pltpu.SMEM, "v": pltpu.VMEM, "a": pl.ANY}
    whole = pl.BlockSpec(memory_space=pltpu.VMEM)
    return pl.pallas_call(
        kernel,
        out_shape=outs,
        in_specs=[pl.BlockSpec(memory_space=places[place]) for place in specs],
        out_specs=out_specs or jax.tree.map(lambda _: whole, outs),
        scratch_shapes=scratch,
        input_output_aliases=aliases or {},
        cost_estimate=pl.CostEstimate(flops=flops, bytes_accessed=1 << 20, transcendentals=0),
        compiler_params=pltpu.CompilerParams(vmem_limit_bytes=limit),
    )


def on_device(acts, preact, cotangent, filt, counts, neighbors):
    slots, voxels, channels = acts.shape
    side = round(voxels ** (1 / 3))
    area = side * side
    spaces = lax.axis_size("space")
    devices = lax.axis_size(AXES)
    rows = filt.shape[0]
    half = (rows + 1) // 2
    padded = -(-half // 16) * 16
    steps = steps_of(spaces, 4)
    flops = 2 * 27 * voxels * channels * channels * slots

    def like(shape, kind):
        return jax.ShapeDtypeStruct(shape, kind)

    shards = filt.T[None]
    low = min(4, spaces)
    gather = [(low * unit, members) for unit, members in reversed(steps_of(spaces // low, 2))]
    gather.append((1, low))

    def gather_start(number, own):
        unit, members = gather[number]
        return [own] + [swapped(own, "space", unit * m) for m in range(members - 1, 0, -1)]

    def gather_finish(arrived, after=(), passed=()):
        own = arrived[0]
        members = len(arrived)
        waits = len(after) + len(passed)
        whole, anywhere = (pl.BlockSpec(memory_space=place) for place in (pltpu.VMEM, pl.ANY))
        return call(
            functools.partial(stack_kernel, members, waits),
            (like((members * own.shape[0],) + own.shape[1:], bf16),)
            + tuple(like(x.shape, x.dtype) for x in passed),
            "v" * members + "a" * waits,
            [],
            10**6,
            out_specs=(whole,) + (anywhere,) * len(passed),
            aliases={members + len(after) + i: 1 + i for i in range(len(passed))},
        )(*arrived, *after, *passed)

    field_shape = like((2 * slots + 1, side, side, side, channels), f32)
    edge_shape = like((slots + 1, 1, side, side, channels), f32)
    sums_shape = like((3 * channels, 9 * channels), f32)
    plane_shape = like((slots, area, channels), bf16)
    buffers = [pltpu.VMEM((voxels, 9 * channels), bf16)] * 2
    turned = [pltpu.VMEM((3 * channels, voxels), bf16)] * 2
    on_the_way = gather_start(0, shards)
    other_neighbors = swapped(neighbors, "rep", 1)
    grads, near, far, acts = call(
        functools.partial(gate_kernel, side),
        (like(acts.shape, bf16), plane_shape, plane_shape, like(acts.shape, bf16)),
        "aaa",
        [pltpu.VMEM(acts.shape, bf16)] * 2 + [pltpu.SemaphoreType.DMA((3, slots))],
        flops // 5,
        limit=50 << 20,
    )(acts, preact, cotangent)
    shards, grads, acts, far = gather_finish(on_the_way, passed=(grads, acts, far))
    other_grads, other_acts = swapped(grads, "rep", 1), swapped(acts, "rep", 1)
    far = with_neighbour(far, 1)
    for number in range(1, len(gather) - 1):
        (shards,) = gather_finish(gather_start(number, shards))
    on_the_way = gather_start(len(gather) - 1, shards)
    sums, field, token = call(
        functools.partial(inner_kernel, side),
        (sums_shape, field_shape, like((8, LANES), f32)),
        "sssvvvva",
        buffers + turned,
        flops,
    )(counts, neighbors, other_neighbors, acts, other_acts, grads, other_grads, shards)
    other_far = swapped(far, "rep", 1)
    (shards,) = gather_finish(on_the_way, (token,))
    other_shards = swapped(shards, "rep", 1)
    mine, sent, low_field, high_field = call(
        functools.partial(outer_kernel, side, rows, half),
        (
            like((spaces, padded, LANES), f32),
            like((spaces * padded + slots * area, LANES), bf16),
            edge_shape,
            edge_shape,
        ),
        "ssvvvva",
        [
            pltpu.VMEM((slots * area, 9 * channels), bf16),
            pltpu.VMEM((slots * area, 9 * channels), bf16),
            pltpu.VMEM((27 * channels + 16, channels), f32),
        ],
        flops // 5,
    )(counts, neighbors, acts, other_grads, far, sums, shards)
    received = swapped(sent, "rep", 1)
    def whole_filter(after):
        return call(
            filter_kernel,
            like((9 * channels, 3 * channels), bf16),
            "vva",
            [pltpu.VMEM((channels, 27 * channels), f32)],
            10**6,
        )(shards, other_shards, after)

    most = (slots + 3) // 4 * 2
    any_place, vector_place = (pl.BlockSpec(memory_space=place) for place in (pl.ANY, pltpu.VMEM))
    scratch = [pltpu.VMEM((voxels + 2 * area, 9 * channels), bf16)] * 2
    scratch += [pltpu.VMEM((voxels + area, 2 * channels), f32)]
    edge_buffer = pltpu.VMEM((2 * slots + 1,) + edge_shape.shape[1:], f32)
    token_shape = like((8, LANES), f32)

    def input_first(wide_filt, after):
        return call(
            functools.partial(input_first_kernel, side, spaces * padded),
            (like((most, voxels, channels), bf16), token_shape),
            "sssvvvvvva",
            [edge_buffer] * 2 + scratch,
            flops // 2,
        )(
            counts, neighbors, other_neighbors, field, low_field, high_field, near, received,
            wide_filt, after,
        )

    def input_rest(wide_filt, done, returned, after):
        return call(
            functools.partial(input_rest_kernel, side),
            (like(acts.shape, bf16), token_shape),
            "ssvvvvvva",
            [pltpu.VMEM((slots + 1, voxels, channels), bf16), pltpu.VMEM((voxels, channels), bf16)]
            + scratch
            + [pltpu.SemaphoreType.DMA((slots,))],
            flops // 2,
            out_specs=(any_place, vector_place),
        )(counts, neighbors, field, low_field, high_field, wide_filt, done, returned, after)

    held, arrived = mine, [received]
    passed, waits = [], []
    for number, (unit, members) in enumerate(steps):
        blocks = held.shape[0] // members
        inputs = [held, *arrived, *passed, *waits]
        outs = call(
            functools.partial(
                reduce_kernel, unit, members, len(arrived), len(passed), len(waits)
            ),
            (like((blocks, padded, LANES), f32),)
            + (like((blocks, padded, LANES), bf16),) * (members - 1)
            + tuple(like(x.shape, x.dtype) for x in passed),
            "v" * (1 + len(arrived)) + "a" * (len(passed) + len(waits)),
            [],
            10**6,
            out_specs=(vector_place,) * members + (any_place,) * len(passed),
            aliases={1 + len(arrived) + i: members + i for i in range(len(passed))},
        )(*inputs)
        held, sends, passed = outs[0], outs[1:members], outs[members:]
        arrived = [swapped(block, "space", unit * (m + 1)) for m, block in enumerate(sends)]
        if number == 0:
            wide_filt = whole_filter(sends[0])
            give, token = input_first(wide_filt, sends[0])
            passed, waits = [give], [token]
        if number == 1:
            returned = swapped(passed[0], "rep", 1)
            input_grad, token = input_rest(wide_filt, passed[0], returned, sends[0])
            passed, waits = [], [token]
    filt_grad = call(
        functools.partial(last_kernel, 1.0 / math.sqrt(slots * devices * voxels), half, len(arrived)),
        like(filt.shape[::-1], f32),
        "v" * (1 + len(arrived)) + "a" * len(waits),
        [],
        10**6,
    )(held, *arrived, *waits)
    return input_grad, filt_grad.T


def solution(mesh):
    in_specs = (
        P(AXES, None, None),
        P(AXES, None, None),
        P(AXES, None, None),
        P("space", "rep"),
        P(),
        P(AXES, None),
    )
    out_specs = (P(AXES, None, None), P("space", "rep"))
    return jax.shard_map(
        on_device, mesh=mesh, in_specs=in_specs, out_specs=out_specs, check_vma=False
    )
```
